256 devices in a mesh: row: 16 (over y, z_hi), col: 16 (over z_lo, x, core).
Axes of the slice: x: 4, y: 4, z: 8 (z_hi: 4, z_lo: 2; z = z_hi * 2 + z_lo), core: 2. Of those that a mesh axis runs over, the one named last changes fastest.
Arguments:
- trail_adj: float32 [16384, 16384], P('row', 'col'), may hold values from -8.5 to 8.5
- panel: float32 [16384, 256], P(('row', 'col')), may hold values from -0.046875 to 0.046875
- panel_adj: float32 [16384, 256], P(('row', 'col')), may hold values from -6 to 6
- diag_inverse: float32 [256, 256], replicated, may hold values from -3 to 2, as said below
- corner_adj: float32 [256, 256], replicated, may hold values from -6 to 6
Outputs:
- solved_adj: float32 [16384, 256], P(('row', 'col'))
- corner: float32 [256, 256], replicated
The draws below stay inside these ranges and needn't reach their ends.
Inputs may be any that keep to these rules, and one draw needn't show every extreme that they name: `diag_inverse`: lower triangular, its diagonal between 1 and 2.
All inputs are finite; a program needn't handle non-finite values.
Results may differ from the reference program's by a relative error of at most 0.00007.
Values sent between devices are 32-bit elements; how exact they have to be, the bound alone decides.
A program may use at most 64 MiB of HBM per device.

```python
import jax
import jax.numpy as jnp
from jax import lax

M = 16384
NB = 256


def draw_trail_adj(key, part):
    key = jax.random.fold_in(key, 11)
    base = jnp.clip(jax.random.normal(key, (M, M), jnp.float32), -6.0, 6.0)
    return (base + base.T) * 0.7071


def draw_diag_inverse(key, part):
    key = jax.random.fold_in(key, 23)
    first, second = jax.random.split(key)
    diagonal = jax.random.uniform(first, (NB,), jnp.float32, 1.0, 2.0)
    lower = jnp.clip(jax.random.normal(second, (NB, NB), jnp.float32), -5.0, 5.0) * (0.8 / NB ** 0.5)
    rows_idx = jnp.arange(NB)[:, None]
    cols_idx = jnp.arange(NB)[None, :]
    lower = jnp.clip(jnp.where(rows_idx > cols_idx, lower, 0.0), -3.0, 2.0)
    return lower + jnp.diag(diagonal)


def steps_of(stream_key, extent, pieces, low, top_value):
    level = 1.0
    for axis_at, shards_of in pieces:
        steps = jax.random.uniform(jax.random.fold_in(jax.random.fold_in(stream_key, 6), axis_at), (shards_of,), jnp.float32, low / len(pieces), top_value / len(pieces))
        level = level * jnp.repeat(jnp.exp(steps), extent[axis_at] // shards_of).reshape((-1,) + (1,) * (len(extent) - 1 - axis_at))
    return level


def normal_values(key, dims, spread, most, pieces=(), held_as=jnp.bfloat16):
    gain = steps_of(key, dims, pieces, -0.22, 0.18) if pieces else 1.0
    values = jax.random.normal(key, dims, jnp.float32) * spread * gain
    return jnp.minimum(jnp.maximum(values, -most), most).astype(held_as)


def setup_inputs(seed: int = 0) -> dict:
    keys = jax.random.split(jax.random.key(seed), 6)
    trail_adj = draw_trail_adj(jax.random.fold_in(keys[5], 71), 0)
    panel = normal_values(keys[1], (M, NB), M ** -0.5, 0.046875, ((0, 256),), jnp.float32)
    panel_adj = normal_values(keys[2], (M, NB), 1.0, 6.0, ((0, 256),), jnp.float32)
    diag_inverse = draw_diag_inverse(jax.random.fold_in(keys[5], 71), 0)
    corner_adj = normal_values(keys[4], (NB, NB), 1.0, 6.0, (), jnp.float32)
    return {"trail_adj": trail_adj, "panel": panel, "panel_adj": panel_adj, "diag_inverse": diag_inverse, "corner_adj": corner_adj}


def reference(trail_adj, panel, panel_adj, diag_inverse, corner_adj):
    highest = lax.Precision.HIGHEST
    product = jnp.dot(trail_adj, panel, precision=highest, preferred_element_type=jnp.float32)
    updated = panel_adj - 2.0 * product
    solved_adj = jnp.dot(updated, diag_inverse, precision=highest, preferred_element_type=jnp.float32)
    corner = corner_adj - jnp.dot(solved_adj.T, panel, precision=highest, preferred_element_type=jnp.float32)
    return solved_adj, corner
```

```python
import functools

import jax
import jax.numpy as jnp
from jax import lax
from jax.experimental import pallas as pl
from jax.experimental.pallas import tpu as pltpu
from jax.sharding import PartitionSpec as P

MESH = pl.DeviceIdType.MESH
F32 = jnp.float32
BF16 = jnp.bfloat16


def split(value):
    high = value.astype(BF16)
    return high, (value - high.astype(F32)).astype(BF16)


def dot3(a_high, a_low, b_high, b_low):
    dot = functools.partial(jnp.dot, preferred_element_type=F32)
    return dot(a_high, b_high) + (dot(a_high, b_low) + dot(a_low, b_high))


def kernel(
    t_hbm, p_hbm, a_hbm, d_hbm, c_hbm, solved_ref, corner_ref,
    t_raw, t_high, t_low, p_own, a_own, d_raw, c_raw, d_high, d_low,
    p_col, p_row, pt_high, pt_low, product,
    sibling, pair_sum, pair_in, m_own, m_in, m_sum, m_plane, md_own, md,
    local_sem, spread_send, col_recv, relay_send,
    row_send, row_fwd, row_recv, sib_send, sib_recv, pair_send, pair_recv,
    m_send, m_recv, z_send, z_recv, out_send, out_recv,
):
    row, col = lax.axis_index("row"), lax.axis_index("col")
    y, z_hi = row // 4, lax.rem(row, 4)
    z_lo, in_plane, core = col // 8, lax.rem(col, 8), lax.rem(col, 2)
    chip = col // 2
    z = z_hi * 2 + z_lo
    place = y * 8 + in_plane
    own_quarter, own_eighth = col // 4, lax.rem(col, 4)

    def in_plane_id(which):
        return ((which // 8) * 4 + z_hi, z_lo * 8 + lax.rem(which, 8))

    def z_id(which):
        return (y * 4 + which // 2, lax.rem(which, 2) * 8 + in_plane)

    slabs = [
        pltpu.make_async_copy(
            t_hbm.at[pl.ds(256 * i, 256)], t_raw.at[pl.ds(256 * i, 256)], local_sem.at[i]
        )
        for i in range(4)
    ]
    p_copy = pltpu.make_async_copy(p_hbm, p_own, local_sem.at[4])
    a_copy = pltpu.make_async_copy(a_hbm, a_own, local_sem.at[5])
    d_copy = pltpu.make_async_copy(d_hbm, d_raw, local_sem.at[6])
    c_copy = pltpu.make_async_copy(c_hbm, c_raw, local_sem.at[7])
    for copy in [p_copy, a_copy] + slabs + [d_copy, c_copy]:
        copy.start()

    barrier = pltpu.get_barrier_semaphore()

    def greet(device_id):
        pl.semaphore_signal(barrier, inc=1, device_id=device_id, device_id_type=MESH)

    diagonal = row == col
    for i in range(4):
        @pl.when(jnp.logical_not(jnp.logical_and(diagonal, own_eighth == i)))
        def _(i=i):
            greet((col, y * 4 + i))

    @pl.loop(1, 8)
    def _(step):
        greet(z_id(lax.rem(z + step, 8)))

    @pl.loop(1, 8)
    def _(step):
        greet((row, lax.rem(chip + step, 8) * 2 + core))

    @pl.loop(1, 32)
    def _(step):
        greet(in_plane_id(lax.rem(place + step, 32)))

    p_copy.wait()
    a_copy.wait()
    p_high, p_low = split(p_own[...])
    a_high, a_low = split(a_own[...])
    m_own[...] = dot3(p_high.T, p_low.T, a_high, a_low).reshape(32, 8, 256)
    p_row[col] = p_own[...]
    for i in range(4):
        slabs[i].wait()

        @pl.loop(0, 4)
        def _(j, i=i):
            rows = pl.ds(256 * i, 256)
            high, low = split(t_raw[rows, pl.ds(pl.multiple_of(256 * j, 256), 256)])
            t_high[j, rows] = high
            t_low[j, rows] = low

    d_copy.wait()
    high, low = split(d_raw[...])
    d_high[...] = high
    d_low[...] = low

    pl.semaphore_wait(barrier, 4 + 7 + 7 + 31 - diagonal.astype(jnp.int32))

    def spread(i):
        return pltpu.make_async_remote_copy(
            src_ref=p_own,
            dst_ref=p_col.at[own_quarter, pl.ds(pl.multiple_of(64 * own_eighth, 64), 64)],
            send_sem=spread_send.at[i],
            recv_sem=col_recv.at[own_quarter, own_eighth],
            device_id=(own_quarter * 4 + i, row),
            device_id_type=MESH,
        )

    def spread_self():
        return pltpu.make_async_copy(
            p_own,
            p_col.at[own_quarter, pl.ds(pl.multiple_of(64 * own_eighth, 64), 64)],
            col_recv.at[own_quarter, own_eighth],
        )

    for i in range(4):
        to_self = jnp.logical_and(diagonal, z_hi == i)

        @pl.when(to_self)
        def _():
            spread_self().start()

        @pl.when(jnp.logical_not(to_self))
        def _(i=i):
            spread(i).start()

    def relay(i, step):
        piece = p_col.at[y, pl.ds(64 * i, 64)]
        return pltpu.make_async_remote_copy(
            src_ref=piece,
            dst_ref=piece,
            send_sem=relay_send.at[i, step - 1],
            recv_sem=col_recv.at[y, i],
            device_id=(lax.rem(y + step, 4) * 4 + z_hi, col),
            device_id_type=MESH,
        )

    def arrived(quarter, i):
        piece = p_col.at[quarter, pl.ds(64 * i, 64)]
        pltpu.make_async_copy(p_own, piece, col_recv.at[quarter, i]).wait()

    for i in range(4):
        arrived(y, i)
        for step in (2, 1, 3):
            relay(i, step).start()

    def to_row(step):
        return pltpu.make_async_remote_copy(
            src_ref=p_own,
            dst_ref=p_row.at[col],
            send_sem=row_send.at[step],
            recv_sem=row_recv.at[col],
            device_id=(row, lax.rem(chip + step, 8) * 2 + core),
            device_id_type=MESH,
        )

    def to_sibling(step):
        block = p_row.at[lax.rem(chip + step, 8) * 2 + core]
        return pltpu.make_async_remote_copy(
            src_ref=block,
            dst_ref=block,
            send_sem=row_fwd.at[step],
            recv_sem=row_recv.at[lax.rem(chip + step, 8) * 2 + core],
            device_id=(row, chip * 2 + 1 - core),
            device_id_type=MESH,
        )

    @pl.loop(1, 8)
    def _(step):
        to_row(step).start()

    to_sibling(0).start()

    def add_quarter(quarter, first):
        high, low = split(p_col[quarter])

        @pl.loop(0, 4)
        def _(i):
            rows = pl.ds(pl.multiple_of(256 * i, 256), 256)
            term = dot3(t_high[quarter, rows], t_low[quarter, rows], high, low)
            place = pl.ds(2 * i, 2)
            term = term.reshape(2, 2, 64, 256)
            product[place] = term if first else product[place] + term

    add_quarter(y, True)

    @pl.loop(1, 8)
    def _(step):
        block = p_row.at[lax.rem(chip + step, 8) * 2 + core]
        pltpu.make_async_copy(p_own, block, row_recv.at[lax.rem(chip + step, 8) * 2 + core]).wait()
        to_sibling(step).start()

    for step in (1, 3):
        quarter = lax.rem(y + step, 4)
        for i in range(4):
            arrived(quarter, i)
        add_quarter(quarter, False)

    @pl.loop(0, 8)
    def _(step):
        which = step * 2 + 1 - core
        pltpu.make_async_copy(p_own, p_row.at[which], row_recv.at[which]).wait()

    for i in range(4):
        high, low = split(p_row[pl.ds(4 * i, 4)].reshape(256, 256))
        pt_high[:, pl.ds(256 * i, 256)] = high.T
        pt_low[:, pl.ds(256 * i, 256)] = low.T

    quarter = lax.rem(y + 2, 4)
    for i in range(4):
        arrived(quarter, i)
    add_quarter(quarter, False)

    total = jnp.zeros((256, 256), F32)
    for i in range(4):
        high, low = split(product[pl.ds(2 * i, 2)].reshape(256, 256))
        total += dot3(pt_high[:, pl.ds(256 * i, 256)], pt_low[:, pl.ds(256 * i, 256)], high, low)
    m_own[...] = m_own[...] - 2.0 * total.reshape(32, 8, 256)
    m_in[place] = m_own[place]

    def to_plane(step):
        which = lax.rem(place + step, 32)
        return pltpu.make_async_remote_copy(
            src_ref=m_own.at[which],
            dst_ref=m_in.at[place],
            send_sem=m_send.at[step],
            recv_sem=m_recv.at[place],
            device_id=in_plane_id(which),
            device_id_type=MESH,
        )

    @pl.loop(1, 32)
    def _(step):
        to_plane(step).start()

    to_pair = pltpu.make_async_remote_copy(
        src_ref=product.at[:, 1 - core],
        dst_ref=sibling,
        send_sem=sib_send,
        recv_sem=sib_recv,
        device_id=(row, chip * 2 + 1 - core),
        device_id_type=MESH,
    )
    to_pair.start()
    to_pair.wait_recv()
    for i in range(8):
        pair_sum[i] = product[i, core] + sibling[i]

    def to_chip(step):
        which = lax.rem(chip + step, 8)
        return pltpu.make_async_remote_copy(
            src_ref=pair_sum.at[which],
            dst_ref=pair_in.at[chip],
            send_sem=pair_send.at[step],
            recv_sem=pair_recv.at[chip],
            device_id=(row, which * 2 + core),
            device_id_type=MESH,
        )

    @pl.loop(1, 8)
    def _(step):
        to_chip(step).start()

    @pl.loop(1, 32)
    def _(step):
        which = lax.rem(place + step, 32)
        pltpu.make_async_copy(md_own, m_in.at[which], m_recv.at[which]).wait()

    total = m_in[0]
    for i in range(1, 32):
        total += m_in[i]
    m_sum[...] = total
    m_plane[z] = total

    def to_z(step):
        return pltpu.make_async_remote_copy(
            src_ref=m_sum,
            dst_ref=m_plane.at[z],
            send_sem=z_send.at[step],
            recv_sem=z_recv.at[z],
            device_id=z_id(lax.rem(z + step, 8)),
            device_id_type=MESH,
        )

    @pl.loop(1, 8)
    def _(step):
        to_z(step).start()

    @pl.loop(1, 8)
    def _(step):
        which = lax.rem(z + step, 8)
        pltpu.make_async_copy(md_own, m_plane.at[which], z_recv.at[which]).wait()

    total = m_plane[0]
    for i in range(1, 8):
        total += m_plane[i]
    high, low = split(jnp.concatenate([total, total], axis=0))
    total = dot3(high, low, d_high[...], d_low[...])[0:8]
    md_own[...] = total
    md[place] = total

    def to_all(step):
        return pltpu.make_async_remote_copy(
            src_ref=md_own,
            dst_ref=md.at[place],
            send_sem=out_send.at[step],
            recv_sem=out_recv.at[place],
            device_id=in_plane_id(lax.rem(place + step, 32)),
            device_id_type=MESH,
        )

    @pl.loop(1, 32)
    def _(step):
        to_all(step).start()

    @pl.loop(1, 8)
    def _(step):
        which = lax.rem(chip + step, 8)
        pltpu.make_async_copy(p_own, pair_in.at[which], pair_recv.at[which]).wait()

    reduced = pair_sum[chip]
    for step in range(1, 8):
        reduced += pair_in[lax.rem(chip + step, 8)]
    high, low = split(a_own[...] - 2.0 * reduced)
    solved_ref[...] = dot3(high, low, d_high[...], d_low[...])
    c_copy.wait()

    for i in range(4):
        @pl.when(jnp.logical_not(jnp.logical_and(diagonal, z_hi == i)))
        def _(i=i):
            spread(i).wait_send()

        for step in (1, 2, 3):
            relay(i, step).wait_send()
    to_sibling(0).wait_send()
    to_pair.wait_send()

    @pl.loop(1, 8)
    def _(step):
        to_row(step).wait_send()
        to_sibling(step).wait_send()
        to_chip(step).wait_send()
        to_z(step).wait_send()

    @pl.loop(1, 32)
    def _(step):
        to_plane(step).wait_send()

    @pl.loop(1, 32)
    def _(step):
        which = lax.rem(place + step, 32)
        pltpu.make_async_copy(md_own, md.at[which], out_recv.at[which]).wait()

    corner_ref[...] = c_raw[...] - md[...].reshape(256, 256).T

    @pl.loop(1, 32)
    def _(step):
        to_all(step).wait_send()


def body(trail_adj, panel, panel_adj, diag_inverse, corner_adj):
    hbm = pl.BlockSpec(memory_space=pl.ANY)
    vmem = pl.BlockSpec(memory_space=pltpu.VMEM)
    dma = pltpu.SemaphoreType.DMA
    return pl.pallas_call(
        kernel,
        out_shape=(
            jax.ShapeDtypeStruct((64, 256), F32),
            jax.ShapeDtypeStruct((256, 256), F32),
        ),
        in_specs=[hbm] * 5,
        out_specs=(vmem, vmem),
        scratch_shapes=[
            pltpu.VMEM((1024, 1024), F32),
            pltpu.VMEM((4, 1024, 256), BF16),
            pltpu.VMEM((4, 1024, 256), BF16),
            pltpu.VMEM((64, 256), F32),
            pltpu.VMEM((64, 256), F32),
            pltpu.VMEM((256, 256), F32),
            pltpu.VMEM((256, 256), F32),
            pltpu.VMEM((256, 256), BF16),
            pltpu.VMEM((256, 256), BF16),
            pltpu.VMEM((4, 256, 256), F32),
            pltpu.VMEM((16, 64, 256), F32),
            pltpu.VMEM((256, 1024), BF16),
            pltpu.VMEM((256, 1024), BF16),
            pltpu.VMEM((8, 2, 64, 256), F32),
            pltpu.VMEM((8, 64, 256), F32),
            pltpu.VMEM((8, 64, 256), F32),
            pltpu.VMEM((8, 64, 256), F32),
            pltpu.VMEM((32, 8, 256), F32),
            pltpu.VMEM((32, 8, 256), F32),
            pltpu.VMEM((8, 256), F32),
            pltpu.VMEM((8, 8, 256), F32),
            pltpu.VMEM((8, 256), F32),
            pltpu.VMEM((32, 8, 256), F32),
            dma((8,)),
            dma((4,)),
            dma((4, 4)),
            dma((4, 3)),
            dma((8,)),
            dma((8,)),
            dma((16,)),
            dma(()),
            dma(()),
            dma((8,)),
            dma((8,)),
            dma((32,)),
            dma((32,)),
            dma((8,)),
            dma((8,)),
            dma((32,)),
            dma((32,)),
        ],
        compiler_params=pltpu.CompilerParams(
            collective_id=0, has_side_effects=True, vmem_limit_bytes=40 * 1024 * 1024
        ),
        name="adjoint_panel",
    )(trail_adj, panel, panel_adj, diag_inverse, corner_adj)


def solution(mesh):
    placed = (P("row", "col"), P(("row", "col"), None), P(("row", "col"), None), P(), P())
    return jax.shard_map(
        body, mesh=mesh, in_specs=placed, out_specs=(P(("row", "col"), None), P()), check_vma=False
    )
```

```python
import functools

import jax
import jax.numpy as jnp
from jax import lax
from jax.experimental import pallas as pl
from jax.experimental.pallas import tpu as pltpu
from jax.sharding import PartitionSpec as P

MESH = pl.DeviceIdType.MESH
F32 = jnp.float32
BF16 = jnp.bfloat16


def split(value):
    high = value.astype(BF16)
    return high, (value - high.astype(F32)).astype(BF16)


def dot3(a_high, a_low, b_high, b_low):
    dot = functools.partial(jnp.dot, preferred_element_type=F32)
    return dot(a_high, b_high) + (dot(a_high, b_low) + dot(a_low, b_high))


def kernel(
    t_hbm, p_hbm, a_hbm, d_hbm, c_hbm, solved_ref, corner_ref,
    t_raw, t_high, t_low, p_own, a_own, d_raw, c_raw, d_high, d_low,
    p_col, p_row, pt_high, pt_low, product,
    sibling, pair_sum, pair_in, m_own, m_in, m_sum, m_plane, md_own, md,
    local_sem, spread_send, col_recv, turn_send, relay_send,
    row_send, row_fwd, row_recv, sib_send, sib_recv, pair_send, pair_recv,
    m_send, m_recv, z_send, z_recv, out_send, out_recv,
):
    row, col = lax.axis_index("row"), lax.axis_index("col")
    y, z_hi = row // 4, lax.rem(row, 4)
    z_lo, in_plane, core = col // 8, lax.rem(col, 8), lax.rem(col, 2)
    chip = col // 2
    z = z_hi * 2 + z_lo
    place = y * 8 + in_plane
    own_quarter, own_piece = col // 4, lax.rem(col, 4)
    odd = lax.rem(z_hi, 2)

    def in_plane_id(which):
        return ((which // 8) * 4 + z_hi, z_lo * 8 + lax.rem(which, 8))

    def z_id(which):
        return (y * 4 + which // 2, lax.rem(which, 2) * 8 + in_plane)

    slabs = [
        pltpu.make_async_copy(
            t_hbm.at[pl.ds(256 * i, 256)], t_raw.at[pl.ds(256 * i, 256)], local_sem.at[i]
        )
        for i in range(4)
    ]
    p_copy = pltpu.make_async_copy(p_hbm, p_own, local_sem.at[4])
    a_copy = pltpu.make_async_copy(a_hbm, a_own, local_sem.at[5])
    d_copy = pltpu.make_async_copy(d_hbm, d_raw, local_sem.at[6])
    c_copy = pltpu.make_async_copy(c_hbm, c_raw, local_sem.at[7])
    for copy in [p_copy, a_copy] + slabs + [d_copy, c_copy]:
        copy.start()

    barrier = pltpu.get_barrier_semaphore()

    def greet(device_id):
        pl.semaphore_signal(barrier, inc=1, device_id=device_id, device_id_type=MESH)

    diagonal = row == col
    for i in range(2):
        @pl.when(jnp.logical_not(jnp.logical_and(diagonal, z_hi // 2 == i)))
        def _(i=i):
            greet((col, y * 4 + odd + 2 * i))

    @pl.loop(1, 8)
    def _(step):
        greet(z_id(lax.rem(z + step, 8)))

    @pl.loop(1, 8)
    def _(step):
        greet((row, lax.rem(chip + step, 8) * 2 + core))

    @pl.loop(1, 32)
    def _(step):
        greet(in_plane_id(lax.rem(place + step, 32)))

    p_copy.wait()
    a_copy.wait()
    p_high, p_low = split(p_own[...])
    a_high, a_low = split(a_own[...])
    m_own[...] = dot3(p_high.T, p_low.T, a_high, a_low).reshape(32, 8, 256)
    p_row[col] = p_own[...]
    for i in range(4):
        slabs[i].wait()

        @pl.loop(0, 4)
        def _(j, i=i):
            rows = pl.ds(256 * i, 256)
            high, low = split(t_raw[rows, pl.ds(pl.multiple_of(256 * j, 256), 256)])
            t_high[j, rows] = high
            t_low[j, rows] = low

    d_copy.wait()
    high, low = split(d_raw[...])
    d_high[...] = high
    d_low[...] = low

    pl.semaphore_wait(barrier, 2 + 7 + 7 + 31 - diagonal.astype(jnp.int32))

    def spread(i):
        return pltpu.make_async_remote_copy(
            src_ref=p_own,
            dst_ref=p_col.at[own_quarter, pl.ds(pl.multiple_of(64 * own_piece, 64), 64)],
            send_sem=spread_send.at[i],
            recv_sem=col_recv.at[own_quarter, own_piece],
            device_id=(own_quarter * 4 + lax.rem(own_piece, 2) + 2 * i, row),
            device_id_type=MESH,
        )

    def spread_self():
        return pltpu.make_async_copy(
            p_own,
            p_col.at[own_quarter, pl.ds(pl.multiple_of(64 * own_piece, 64), 64)],
            col_recv.at[own_quarter, own_piece],
        )

    for i in range(2):
        to_self = jnp.logical_and(diagonal, z_hi // 2 == i)

        @pl.when(to_self)
        def _():
            spread_self().start()

        @pl.when(jnp.logical_not(to_self))
        def _(i=i):
            spread(i).start()

    pieces = (odd, odd + 2, 1 - odd, 3 - odd)

    def turn(i):
        which = pieces[i]
        piece = p_col.at[y, pl.ds(pl.multiple_of(64 * which, 64), 64)]
        return pltpu.make_async_remote_copy(
            src_ref=piece,
            dst_ref=piece,
            send_sem=turn_send.at[i],
            recv_sem=col_recv.at[y, which],
            device_id=(y * 4 + lax.rem(z_hi + 1 + 2 * i, 4), col),
            device_id_type=MESH,
        )

    def relay(i, step):
        which = pieces[i]
        piece = p_col.at[y, pl.ds(pl.multiple_of(64 * which, 64), 64)]
        return pltpu.make_async_remote_copy(
            src_ref=piece,
            dst_ref=piece,
            send_sem=relay_send.at[i, step - 1],
            recv_sem=col_recv.at[y, which],
            device_id=(lax.rem(y + step, 4) * 4 + z_hi, col),
            device_id_type=MESH,
        )

    def arrived(quarter, i):
        piece = p_col.at[quarter, pl.ds(pl.multiple_of(64 * i, 64), 64)]
        pltpu.make_async_copy(p_own, piece, col_recv.at[quarter, i]).wait()

    for i in range(4):
        arrived(y, pieces[i])
        if i < 2:
            turn(i).start()
        for step in (2, 1, 3):
            relay(i, step).start()

    def to_row(step):
        return pltpu.make_async_remote_copy(
            src_ref=p_own,
            dst_ref=p_row.at[col],
            send_sem=row_send.at[step],
            recv_sem=row_recv.at[col],
            device_id=(row, lax.rem(chip + step, 8) * 2 + core),
            device_id_type=MESH,
        )

    def to_sibling(step):
        block = p_row.at[lax.rem(chip + step, 8) * 2 + core]
        return pltpu.make_async_remote_copy(
            src_ref=block,
            dst_ref=block,
            send_sem=row_fwd.at[step],
            recv_sem=row_recv.at[lax.rem(chip + step, 8) * 2 + core],
            device_id=(row, chip * 2 + 1 - core),
            device_id_type=MESH,
        )

    @pl.loop(1, 8)
    def _(step):
        to_row(step).start()

    to_sibling(0).start()

    def add_quarter(quarter, first):
        high, low = split(p_col[quarter])

        @pl.loop(0, 4)
        def _(i):
            rows = pl.ds(pl.multiple_of(256 * i, 256), 256)
            term = dot3(t_high[quarter, rows], t_low[quarter, rows], high, low)
            place = pl.ds(2 * i, 2)
            term = term.reshape(2, 2, 64, 256)
            product[place] = term if first else product[place] + term

    add_quarter(y, True)

    @pl.loop(1, 8)
    def _(step):
        block = p_row.at[lax.rem(chip + step, 8) * 2 + core]
        pltpu.make_async_copy(p_own, block, row_recv.at[lax.rem(chip + step, 8) * 2 + core]).wait()
        to_sibling(step).start()

    for step in (1, 3):
        quarter = lax.rem(y + step, 4)
        for i in range(4):
            arrived(quarter, i)
        add_quarter(quarter, False)

    @pl.loop(0, 8)
    def _(step):
        which = step * 2 + 1 - core
        pltpu.make_async_copy(p_own, p_row.at[which], row_recv.at[which]).wait()

    for i in range(4):
        high, low = split(p_row[pl.ds(4 * i, 4)].reshape(256, 256))
        pt_high[:, pl.ds(256 * i, 256)] = high.T
        pt_low[:, pl.ds(256 * i, 256)] = low.T

    quarter = lax.rem(y + 2, 4)
    for i in range(4):
        arrived(quarter, i)
    add_quarter(quarter, False)

    total = jnp.zeros((256, 256), F32)
    for i in range(4):
        high, low = split(product[pl.ds(2 * i, 2)].reshape(256, 256))
        total += dot3(pt_high[:, pl.ds(256 * i, 256)], pt_low[:, pl.ds(256 * i, 256)], high, low)
    m_own[...] = m_own[...] - 2.0 * total.reshape(32, 8, 256)
    m_in[place] = m_own[place]

    def to_plane(step):
        which = lax.rem(place + step, 32)
        return pltpu.make_async_remote_copy(
            src_ref=m_own.at[which],
            dst_ref=m_in.at[place],
            send_sem=m_send.at[step],
            recv_sem=m_recv.at[place],
            device_id=in_plane_id(which),
            device_id_type=MESH,
        )

    @pl.loop(1, 32)
    def _(step):
        to_plane(step).start()

    to_pair = pltpu.make_async_remote_copy(
        src_ref=product.at[:, 1 - core],
        dst_ref=sibling,
        send_sem=sib_send,
        recv_sem=sib_recv,
        device_id=(row, chip * 2 + 1 - core),
        device_id_type=MESH,
    )
    to_pair.start()
    to_pair.wait_recv()
    for i in range(8):
        pair_sum[i] = product[i, core] + sibling[i]

    def to_chip(step):
        which = lax.rem(chip + step, 8)
        return pltpu.make_async_remote_copy(
            src_ref=pair_sum.at[which],
            dst_ref=pair_in.at[chip],
            send_sem=pair_send.at[step],
            recv_sem=pair_recv.at[chip],
            device_id=(row, which * 2 + core),
            device_id_type=MESH,
        )

    @pl.loop(1, 32)
    def _(step):
        which = lax.rem(place + step, 32)
        pltpu.make_async_copy(md_own, m_in.at[which], m_recv.at[which]).wait()

    total = m_in[0]
    for i in range(1, 32):
        total += m_in[i]
    m_sum[...] = total
    m_plane[z] = total

    def to_z(step):
        return pltpu.make_async_remote_copy(
            src_ref=m_sum,
            dst_ref=m_plane.at[z],
            send_sem=z_send.at[step],
            recv_sem=z_recv.at[z],
            device_id=z_id(lax.rem(z + step, 8)),
            device_id_type=MESH,
        )

    @pl.loop(1, 8)
    def _(step):
        to_z(step).start()

    @pl.loop(1, 8)
    def _(step):
        to_chip(step).start()

    @pl.loop(1, 8)
    def _(step):
        which = lax.rem(z + step, 8)
        pltpu.make_async_copy(md_own, m_plane.at[which], z_recv.at[which]).wait()

    total = m_plane[0]
    for i in range(1, 8):
        total += m_plane[i]
    high, low = split(jnp.concatenate([total, total], axis=0))
    total = dot3(high, low, d_high[...], d_low[...])[0:8]
    md_own[...] = total
    md[place] = total

    def to_all(step):
        return pltpu.make_async_remote_copy(
            src_ref=md_own,
            dst_ref=md.at[place],
            send_sem=out_send.at[step],
            recv_sem=out_recv.at[place],
            device_id=in_plane_id(lax.rem(place + step, 32)),
            device_id_type=MESH,
        )

    @pl.loop(1, 32)
    def _(step):
        to_all(step).start()

    @pl.loop(1, 8)
    def _(step):
        which = lax.rem(chip + step, 8)
        pltpu.make_async_copy(p_own, pair_in.at[which], pair_recv.at[which]).wait()

    reduced = pair_sum[chip]
    for step in range(1, 8):
        reduced += pair_in[lax.rem(chip + step, 8)]
    high, low = split(a_own[...] - 2.0 * reduced)
    solved_ref[...] = dot3(high, low, d_high[...], d_low[...])
    c_copy.wait()

    for i in range(2):
        @pl.when(jnp.logical_not(jnp.logical_and(diagonal, z_hi // 2 == i)))
        def _(i=i):
            spread(i).wait_send()

        turn(i).wait_send()

    for i in range(4):
        for step in (1, 2, 3):
            relay(i, step).wait_send()
    to_sibling(0).wait_send()
    to_pair.wait_send()

    @pl.loop(1, 8)
    def _(step):
        to_row(step).wait_send()
        to_sibling(step).wait_send()
        to_chip(step).wait_send()
        to_z(step).wait_send()

    @pl.loop(1, 32)
    def _(step):
        to_plane(step).wait_send()

    @pl.loop(1, 32)
    def _(step):
        which = lax.rem(place + step, 32)
        pltpu.make_async_copy(md_own, md.at[which], out_recv.at[which]).wait()

    corner_ref[...] = c_raw[...] - md[...].reshape(256, 256).T

    @pl.loop(1, 32)
    def _(step):
        to_all(step).wait_send()


def body(trail_adj, panel, panel_adj, diag_inverse, corner_adj):
    hbm = pl.BlockSpec(memory_space=pl.ANY)
    vmem = pl.BlockSpec(memory_space=pltpu.VMEM)
    dma = pltpu.SemaphoreType.DMA
    return pl.pallas_call(
        kernel,
        out_shape=(
            jax.ShapeDtypeStruct((64, 256), F32),
            jax.ShapeDtypeStruct((256, 256), F32),
        ),
        in_specs=[hbm] * 5,
        out_specs=(vmem, vmem),
        scratch_shapes=[
            pltpu.VMEM((1024, 1024), F32),
            pltpu.VMEM((4, 1024, 256), BF16),
            pltpu.VMEM((4, 1024, 256), BF16),
            pltpu.VMEM((64, 256), F32),
            pltpu.VMEM((64, 256), F32),
            pltpu.VMEM((256, 256), F32),
            pltpu.VMEM((256, 256), F32),
            pltpu.VMEM((256, 256), BF16),
            pltpu.VMEM((256, 256), BF16),
            pltpu.VMEM((4, 256, 256), F32),
            pltpu.VMEM((16, 64, 256), F32),
            pltpu.VMEM((256, 1024), BF16),
            pltpu.VMEM((256, 1024), BF16),
            pltpu.VMEM((8, 2, 64, 256), F32),
            pltpu.VMEM((8, 64, 256), F32),
            pltpu.VMEM((8, 64, 256), F32),
            pltpu.VMEM((8, 64, 256), F32),
            pltpu.VMEM((32, 8, 256), F32),
            pltpu.VMEM((32, 8, 256), F32),
            pltpu.VMEM((8, 256), F32),
            pltpu.VMEM((8, 8, 256), F32),
            pltpu.VMEM((8, 256), F32),
            pltpu.VMEM((32, 8, 256), F32),
            dma((8,)),
            dma((4,)),
            dma((4, 4)),
            dma((2,)),
            dma((4, 3)),
            dma((8,)),
            dma((8,)),
            dma((16,)),
            dma(()),
            dma(()),
            dma((8,)),
            dma((8,)),
            dma((32,)),
            dma((32,)),
            dma((8,)),
            dma((8,)),
            dma((32,)),
            dma((32,)),
        ],
        compiler_params=pltpu.CompilerParams(
            collective_id=0, has_side_effects=True, vmem_limit_bytes=60 * 1024 * 1024
        ),
        name="adjoint_panel",
    )(trail_adj, panel, panel_adj, diag_inverse, corner_adj)


def solution(mesh):
    placed = (P("row", "col"), P(("row", "col"), None), P(("row", "col"), None), P(), P())
    return jax.shard_map(
        body, mesh=mesh, in_specs=placed, out_specs=(P(("row", "col"), None), P()), check_vma=False
    )
```

```python
import functools

import jax
import jax.numpy as jnp
from jax import lax
from jax.experimental import pallas as pl
from jax.experimental.pallas import tpu as pltpu
from jax.sharding import PartitionSpec as P

MESH = pl.DeviceIdType.MESH
F32 = jnp.float32
BF16 = jnp.bfloat16


def split(value):
    high = value.astype(BF16)
    return high, (value - high.astype(F32)).astype(BF16)


def dot3(a_high, a_low, b_high, b_low):
    dot = functools.partial(jnp.dot, preferred_element_type=F32)
    return dot(a_high, b_high) + (dot(a_high, b_low) + dot(a_low, b_high))


def kernel(
    t_hbm, p_hbm, a_hbm, d_hbm, c_hbm, solved_ref, corner_ref,
    t_raw, t_high, t_low, p_own, a_own, d_raw, c_raw, d_high, d_low,
    p_col, p_row, pt_high, pt_low, pt_t_high, pt_t_low, p_col_high, p_col_low, product,
    sibling, pair_sum, pair_in, m_own, m_in, m_sum, m_plane, md_own, md,
    local_sem, spread_send, col_recv, turn_send, relay_send,
    row_send, row_fwd, row_recv, sib_send, sib_recv, pair_send, pair_recv,
    m_send, m_recv, z_send, z_recv, out_send, out_recv,
):
    row, col = lax.axis_index("row"), lax.axis_index("col")
    y, z_hi = row // 4, lax.rem(row, 4)
    z_lo, in_plane, core = col // 8, lax.rem(col, 8), lax.rem(col, 2)
    chip = col // 2
    z = z_hi * 2 + z_lo
    place = y * 8 + in_plane
    own_quarter, own_piece = col // 4, lax.rem(col, 4)
    odd = lax.rem(z_hi, 2)

    def in_plane_id(which):
        return ((which // 8) * 4 + z_hi, z_lo * 8 + lax.rem(which, 8))

    def z_id(which):
        return (y * 4 + which // 2, lax.rem(which, 2) * 8 + in_plane)

    slabs = [
        pltpu.make_async_copy(
            t_hbm.at[pl.ds(256 * i, 256)], t_raw.at[pl.ds(256 * i, 256)], local_sem.at[i]
        )
        for i in range(4)
    ]
    p_copy = pltpu.make_async_copy(p_hbm, p_own, local_sem.at[4])
    a_copy = pltpu.make_async_copy(a_hbm, a_own, local_sem.at[5])
    d_copy = pltpu.make_async_copy(d_hbm, d_raw, local_sem.at[6])
    c_copy = pltpu.make_async_copy(c_hbm, c_raw, local_sem.at[7])
    for copy in [p_copy, a_copy] + slabs + [d_copy, c_copy]:
        copy.start()

    barrier = pltpu.get_barrier_semaphore()

    def greet(device_id):
        pl.semaphore_signal(barrier, inc=1, device_id=device_id, device_id_type=MESH)

    diagonal = row == col
    for i in range(2):
        @pl.when(jnp.logical_not(jnp.logical_and(diagonal, z_hi // 2 == i)))
        def _(i=i):
            greet((col, y * 4 + odd + 2 * i))

    @pl.loop(1, 8)
    def _(step):
        greet(z_id(lax.rem(z + step, 8)))

    @pl.loop(1, 4)
    def _(step):
        greet((row, (1 - z_lo) * 8 + lax.rem(in_plane + 2 * step, 8)))

    @pl.loop(1, 32)
    def _(step):
        greet(in_plane_id(lax.rem(place + step, 32)))

    p_copy.wait()
    a_copy.wait()
    p_high, p_low = split(p_own[...])
    a_high, a_low = split(a_own[...])
    m_own[...] = dot3(p_high.T, p_low.T, a_high, a_low).reshape(32, 8, 256)
    p_row[col] = p_own[...]
    for i in range(4):
        slabs[i].wait()

        @pl.loop(0, 4)
        def _(j, i=i):
            rows = pl.ds(256 * i, 256)
            high, low = split(t_raw[rows, pl.ds(pl.multiple_of(256 * j, 256), 256)])
            t_high[j, rows] = high
            t_low[j, rows] = low

    d_copy.wait()
    high, low = split(d_raw[...])
    d_high[...] = high
    d_low[...] = low

    pl.semaphore_wait(barrier, 2 + 7 + 3 + 31 - diagonal.astype(jnp.int32))

    def spread(i):
        return pltpu.make_async_remote_copy(
            src_ref=p_own,
            dst_ref=p_col.at[own_quarter, pl.ds(pl.multiple_of(64 * own_piece, 64), 64)],
            send_sem=spread_send.at[i],
            recv_sem=col_recv.at[own_quarter, own_piece],
            device_id=(own_quarter * 4 + lax.rem(own_piece, 2) + 2 * i, row),
            device_id_type=MESH,
        )

    def spread_self():
        return pltpu.make_async_copy(
            p_own,
            p_col.at[own_quarter, pl.ds(pl.multiple_of(64 * own_piece, 64), 64)],
            col_recv.at[own_quarter, own_piece],
        )

    for i in range(2):
        to_self = jnp.logical_and(diagonal, z_hi // 2 == i)

        @pl.when(to_self)
        def _():
            spread_self().start()

        @pl.when(jnp.logical_not(to_self))
        def _(i=i):
            spread(i).start()

    pieces = (odd, odd + 2, 1 - odd, 3 - odd)

    def turn(i):
        which = pieces[i]
        piece = p_col.at[y, pl.ds(pl.multiple_of(64 * which, 64), 64)]
        return pltpu.make_async_remote_copy(
            src_ref=piece,
            dst_ref=piece,
            send_sem=turn_send.at[i],
            recv_sem=col_recv.at[y, which],
            device_id=(y * 4 + lax.rem(z_hi + 1 + 2 * i, 4), col),
            device_id_type=MESH,
        )

    def relay(i, step):
        which = pieces[i]
        piece = p_col.at[y, pl.ds(pl.multiple_of(64 * which, 64), 64)]
        return pltpu.make_async_remote_copy(
            src_ref=piece,
            dst_ref=piece,
            send_sem=relay_send.at[i, step - 1],
            recv_sem=col_recv.at[y, which],
            device_id=(lax.rem(y + step, 4) * 4 + z_hi, col),
            device_id_type=MESH,
        )

    def arrived(quarter, i):
        piece = p_col.at[quarter, pl.ds(pl.multiple_of(64 * i, 64), 64)]
        pltpu.make_async_copy(p_own, piece, col_recv.at[quarter, i]).wait()

    def to_partner():
        return pltpu.make_async_remote_copy(
            src_ref=p_own,
            dst_ref=p_row.at[col],
            send_sem=row_send.at[0],
            recv_sem=row_recv.at[col],
            device_id=(row, (1 - z_lo) * 8 + in_plane),
            device_id_type=MESH,
        )

    def to_row(half, step):
        which = lax.rem(z_lo + half, 2) * 8 + in_plane
        block = p_row.at[which]
        return pltpu.make_async_remote_copy(
            src_ref=block,
            dst_ref=block,
            send_sem=row_send.at[half * 4 + step],
            recv_sem=row_recv.at[which],
            device_id=(row, z_lo * 8 + lax.rem(in_plane + 2 * step, 8)),
            device_id_type=MESH,
        )

    def to_sibling(step):
        which = lax.rem(chip + step, 8) * 2 + core
        block = p_row.at[which]
        return pltpu.make_async_remote_copy(
            src_ref=block,
            dst_ref=block,
            send_sem=row_fwd.at[step],
            recv_sem=row_recv.at[which],
            device_id=(row, chip * 2 + 1 - core),
            device_id_type=MESH,
        )

    def row_arrived(which):
        pltpu.make_async_copy(p_own, p_row.at[which], row_recv.at[which]).wait()

    to_partner().start()
    to_sibling(0).start()
    for i in range(4):
        arrived(y, pieces[i])
        if i < 2:
            turn(i).start()
        for step in (2, 1, 3):
            relay(i, step).start()
        if i == 1:
            for step in (2, 1, 3):
                to_row(0, step).start()
            row_arrived((1 - z_lo) * 8 + in_plane)
            for step in (2, 1, 3):
                to_row(1, step).start()
            to_sibling(4).start()

    for step in (1, 2, 3, 5, 6, 7):
        row_arrived(lax.rem(chip + step, 8) * 2 + core)
        to_sibling(step).start()

    for i in range(4):
        for step in (0, 1):
            row_arrived(4 * i + 2 * step + 1 - core)
        high, low = split(p_row[pl.ds(4 * i, 4)].reshape(256, 256))
        pt_high[:, pl.ds(256 * i, 256)] = high.T
        pt_low[:, pl.ds(256 * i, 256)] = low.T

    @pl.loop(0, 4)
    def _(j):
        high, low = split(dot3(pt_high[...], pt_low[...], t_high[j], t_low[j]))
        pt_t_high[j] = high
        pt_t_low[j] = low

    total = jnp.zeros((256, 256), F32)
    for step in (0, 1, 3, 2):
        quarter = lax.rem(y + step, 4)
        if step:
            for i in range(4):
                arrived(quarter, i)
        high, low = split(p_col[quarter])
        p_col_high[quarter] = high
        p_col_low[quarter] = low
        total += dot3(pt_t_high[quarter], pt_t_low[quarter], high, low)
    m_own[...] = m_own[...] - 2.0 * total.reshape(32, 8, 256)
    m_in[place] = m_own[place]

    def to_plane(step):
        which = lax.rem(place + step, 32)
        return pltpu.make_async_remote_copy(
            src_ref=m_own.at[which],
            dst_ref=m_in.at[place],
            send_sem=m_send.at[step],
            recv_sem=m_recv.at[place],
            device_id=in_plane_id(which),
            device_id_type=MESH,
        )

    @pl.loop(1, 32)
    def _(step):
        to_plane(step).start()

    @pl.loop(0, 4)
    def _(i):
        rows = pl.ds(pl.multiple_of(256 * i, 256), 256)
        total = jnp.zeros((256, 256), F32)
        for j in range(4):
            total += dot3(t_high[j, rows], t_low[j, rows], p_col_high[j], p_col_low[j])
        product[pl.ds(2 * i, 2)] = total.reshape(2, 2, 64, 256)

    to_pair = pltpu.make_async_remote_copy(
        src_ref=product.at[:, 1 - core],
        dst_ref=sibling,
        send_sem=sib_send,
        recv_sem=sib_recv,
        device_id=(row, chip * 2 + 1 - core),
        device_id_type=MESH,
    )
    to_pair.start()
    to_pair.wait_recv()
    for i in range(8):
        pair_sum[i] = product[i, core] + sibling[i]

    def to_chip(step):
        which = lax.rem(chip + step, 8)
        return pltpu.make_async_remote_copy(
            src_ref=pair_sum.at[which],
            dst_ref=pair_in.at[chip],
            send_sem=pair_send.at[step],
            recv_sem=pair_recv.at[chip],
            device_id=(row, which * 2 + core),
            device_id_type=MESH,
        )

    @pl.loop(1, 32)
    def _(step):
        which = lax.rem(place + step, 32)
        pltpu.make_async_copy(md_own, m_in.at[which], m_recv.at[which]).wait()

    total = m_in[0]
    for i in range(1, 32):
        total += m_in[i]
    m_sum[...] = total
    m_plane[z] = total

    def to_z(step):
        return pltpu.make_async_remote_copy(
            src_ref=m_sum,
            dst_ref=m_plane.at[z],
            send_sem=z_send.at[step],
            recv_sem=z_recv.at[z],
            device_id=z_id(lax.rem(z + step, 8)),
            device_id_type=MESH,
        )

    @pl.loop(1, 8)
    def _(step):
        to_z(step).start()

    @pl.loop(1, 8)
    def _(step):
        to_chip(step).start()

    @pl.loop(1, 8)
    def _(step):
        which = lax.rem(z + step, 8)
        pltpu.make_async_copy(md_own, m_plane.at[which], z_recv.at[which]).wait()

    total = m_plane[0]
    for i in range(1, 8):
        total += m_plane[i]
    high, low = split(jnp.concatenate([total, total], axis=0))
    total = dot3(high, low, d_high[...], d_low[...])[0:8]
    md_own[...] = total
    md[place] = total

    def to_all(step):
        return pltpu.make_async_remote_copy(
            src_ref=md_own,
            dst_ref=md.at[place],
            send_sem=out_send.at[step],
            recv_sem=out_recv.at[place],
            device_id=in_plane_id(lax.rem(place + step, 32)),
            device_id_type=MESH,
        )

    @pl.loop(1, 32)
    def _(step):
        to_all(step).start()

    @pl.loop(1, 8)
    def _(step):
        which = lax.rem(chip + step, 8)
        pltpu.make_async_copy(p_own, pair_in.at[which], pair_recv.at[which]).wait()

    reduced = pair_sum[chip]
    for step in range(1, 8):
        reduced += pair_in[lax.rem(chip + step, 8)]
    high, low = split(a_own[...] - 2.0 * reduced)
    solved_ref[...] = dot3(high, low, d_high[...], d_low[...])
    c_copy.wait()

    for i in range(2):
        @pl.when(jnp.logical_not(jnp.logical_and(diagonal, z_hi // 2 == i)))
        def _(i=i):
            spread(i).wait_send()

        turn(i).wait_send()

    for i in range(4):
        for step in (1, 2, 3):
            relay(i, step).wait_send()
    to_sibling(0).wait_send()
    to_partner().wait_send()
    for step in (1, 2, 3):
        to_row(0, step).wait_send()
        to_row(1, step).wait_send()
    to_pair.wait_send()

    @pl.loop(1, 8)
    def _(step):
        to_sibling(step).wait_send()
        to_chip(step).wait_send()
        to_z(step).wait_send()

    @pl.loop(1, 32)
    def _(step):
        to_plane(step).wait_send()
        to_all(step).wait_send()

    @pl.loop(1, 32)
    def _(step):
        which = lax.rem(place + step, 32)
        pltpu.make_async_copy(md_own, md.at[which], out_recv.at[which]).wait()

    corner_ref[...] = c_raw[...] - md[...].reshape(256, 256).T


def body(*arrays):
    hbm = pl.BlockSpec(memory_space=pltpu.HBM)
    vmem = pl.BlockSpec(memory_space=pltpu.VMEM)
    dma = pltpu.SemaphoreType.DMA
    return pl.pallas_call(
        kernel,
        out_shape=(
            jax.ShapeDtypeStruct((64, 256), F32),
            jax.ShapeDtypeStruct((256, 256), F32),
        ),
        in_specs=[hbm] * 5,
        out_specs=(vmem, vmem),
        scratch_shapes=[
            pltpu.VMEM((1024, 1024), F32),
            pltpu.VMEM((4, 1024, 256), BF16),
            pltpu.VMEM((4, 1024, 256), BF16),
            pltpu.VMEM((64, 256), F32),
            pltpu.VMEM((64, 256), F32),
            pltpu.VMEM((256, 256), F32),
            pltpu.VMEM((256, 256), F32),
            pltpu.VMEM((256, 256), BF16),
            pltpu.VMEM((256, 256), BF16),
            pltpu.VMEM((4, 256, 256), F32),
            pltpu.VMEM((16, 64, 256), F32),
            pltpu.VMEM((256, 1024), BF16),
            pltpu.VMEM((256, 1024), BF16),
            pltpu.VMEM((4, 256, 256), BF16),
            pltpu.VMEM((4, 256, 256), BF16),
            pltpu.VMEM((4, 256, 256), BF16),
            pltpu.VMEM((4, 256, 256), BF16),
            pltpu.VMEM((8, 2, 64, 256), F32),
            pltpu.VMEM((8, 64, 256), F32),
            pltpu.VMEM((8, 64, 256), F32),
            pltpu.VMEM((8, 64, 256), F32),
            pltpu.VMEM((32, 8, 256), F32),
            pltpu.VMEM((32, 8, 256), F32),
            pltpu.VMEM((8, 256), F32),
            pltpu.VMEM((8, 8, 256), F32),
            pltpu.VMEM((8, 256), F32),
            pltpu.VMEM((32, 8, 256), F32),
            dma((8,)),
            dma((4,)),
            dma((4, 4)),
            dma((2,)),
            dma((4, 3)),
            dma((8,)),
            dma((8,)),
            dma((16,)),
            dma(()),
            dma(()),
            dma((8,)),
            dma((8,)),
            dma((32,)),
            dma((32,)),
            dma((8,)),
            dma((8,)),
            dma((32,)),
            dma((32,)),
        ],
        compiler_params=pltpu.CompilerParams(
            collective_id=0, has_side_effects=True, vmem_limit_bytes=32 * 1024 * 1024
        ),
        name="adjoint_panel",
    )(*(pltpu.with_memory_space_constraint(x, pltpu.HBM) for x in arrays))


def solution(mesh):
    placed = (P("row", "col"), P(("row", "col"), None), P(("row", "col"), None), P(), P())
    return jax.shard_map(
        body, mesh=mesh, in_specs=placed, out_specs=(P(("row", "col"), None), P()), check_vma=False
    )
```

```python
import functools

import jax
import jax.numpy as jnp
from jax import lax
from jax.experimental import pallas as pl
from jax.experimental.pallas import tpu as pltpu
from jax.sharding import PartitionSpec as P

MESH = pl.DeviceIdType.MESH
F32 = jnp.float32
BF16 = jnp.bfloat16


def split(value):
    high = value.astype(BF16)
    return high, (value - high.astype(F32)).astype(BF16)


def dot3(a_high, a_low, b_high, b_low):
    dot = functools.partial(jnp.dot, preferred_element_type=F32)
    return dot(a_high, b_high) + (dot(a_high, b_low) + dot(a_low, b_high))


def kernel(
    t_hbm, p_hbm, a_hbm, d_hbm, c_hbm, solved_ref, corner_ref,
    t_raw, t_high, t_low, p_own, a_own, d_raw, c_raw, d_high, d_low,
    p_col, p_row, pt_high, pt_low, pt_t_high, pt_t_low, p_col_high, p_col_low, product,
    sibling, pair_sum, pair_in, m_own, m_in, m_sum, m_plane, md_own, md,
    local_sem, spread_send, col_recv, z_relay_send, y_relay_send, onward_send,
    row_send, row_fwd, row_recv, sib_send, sib_recv, pair_send, pair_recv,
    m_send, m_recv, z_send, z_recv, out_send, out_recv,
):
    row, col = lax.axis_index("row"), lax.axis_index("col")
    y, z_hi = row // 4, lax.rem(row, 4)
    z_lo, in_plane, core = col // 8, lax.rem(col, 8), lax.rem(col, 2)
    chip = col // 2
    z = z_hi * 2 + z_lo
    place = y * 8 + in_plane
    far_y, far_z, next_z, last_z = (
        lax.rem(y + 2, 4), lax.rem(z_hi + 2, 4), lax.rem(z_hi + 1, 4), lax.rem(z_hi + 3, 4)
    )

    def opposite(which):
        return lax.rem(which // 4 + 2, 4) * 4 + lax.rem(which + 2, 4)

    def in_plane_id(which):
        return ((which // 8) * 4 + z_hi, z_lo * 8 + lax.rem(which, 8))

    def z_id(which):
        return (y * 4 + which // 2, lax.rem(which, 2) * 8 + in_plane)

    slabs = [
        pltpu.make_async_copy(
            t_hbm.at[pl.ds(256 * i, 256)], t_raw.at[pl.ds(256 * i, 256)], local_sem.at[i]
        )
        for i in range(4)
    ]
    p_copy = pltpu.make_async_copy(p_hbm, p_own, local_sem.at[4])
    a_copy = pltpu.make_async_copy(a_hbm, a_own, local_sem.at[5])
    d_copy = pltpu.make_async_copy(d_hbm, d_raw, local_sem.at[6])
    c_copy = pltpu.make_async_copy(c_hbm, c_raw, local_sem.at[7])
    for copy in [p_copy, a_copy] + slabs + [d_copy, c_copy]:
        copy.start()

    barrier = pltpu.get_barrier_semaphore()

    def greet(device_id):
        pl.semaphore_signal(barrier, inc=1, device_id=device_id, device_id_type=MESH)

    diagonal = row == col

    @pl.when(jnp.logical_not(diagonal))
    def _():
        greet((col, row))

    greet((col, opposite(row)))

    @pl.loop(1, 8)
    def _(step):
        greet(z_id(lax.rem(z + step, 8)))

    @pl.loop(1, 4)
    def _(step):
        greet((row, (1 - z_lo) * 8 + lax.rem(in_plane + 2 * step, 8)))

    @pl.loop(1, 32)
    def _(step):
        greet(in_plane_id(lax.rem(place + step, 32)))

    p_copy.wait()
    a_copy.wait()
    p_high, p_low = split(p_own[...])
    a_high, a_low = split(a_own[...])
    m_own[...] = dot3(p_high.T, p_low.T, a_high, a_low).reshape(32, 8, 256)
    p_row[col] = p_own[...]
    for i in range(4):
        slabs[i].wait()

        @pl.loop(0, 4)
        def _(j, i=i):
            rows = pl.ds(256 * i, 256)
            high, low = split(t_raw[rows, pl.ds(pl.multiple_of(256 * j, 256), 256)])
            t_high[j, rows] = high
            t_low[j, rows] = low

    d_copy.wait()
    high, low = split(d_raw[...])
    d_high[...] = high
    d_low[...] = low

    pl.semaphore_wait(barrier, 2 + 7 + 3 + 31 - diagonal.astype(jnp.int32))

    def piece(quarter, which):
        return p_col.at[quarter, pl.ds(pl.multiple_of(64 * which, 64), 64)]

    def arrived(quarter, which):
        pltpu.make_async_copy(p_own, piece(quarter, which), col_recv.at[quarter, which]).wait()

    own_piece = piece(col // 4, lax.rem(col, 4))
    own_recv = col_recv.at[col // 4, lax.rem(col, 4)]

    def spread(i):
        return pltpu.make_async_remote_copy(
            src_ref=p_own,
            dst_ref=own_piece,
            send_sem=spread_send.at[i],
            recv_sem=own_recv,
            device_id=((col, opposite(col))[i], row),
            device_id_type=MESH,
        )

    @pl.when(diagonal)
    def _():
        pltpu.make_async_copy(p_own, own_piece, own_recv).start()

    @pl.when(jnp.logical_not(diagonal))
    def _():
        spread(0).start()

    spread(1).start()

    held = ((y, z_hi), (far_y, far_z))
    passed = ((y, last_z), (far_y, next_z))

    def relay(source, send_sem, to_y, to_z):
        return pltpu.make_async_remote_copy(
            src_ref=piece(*source),
            dst_ref=piece(*source),
            send_sem=send_sem,
            recv_sem=col_recv.at[source[0], source[1]],
            device_id=(to_y * 4 + to_z, col),
            device_id_type=MESH,
        )

    def along_z(i, step):
        return relay(held[i], z_relay_send.at[i, step], y, lax.rem(z_hi + step, 4))

    def along_y(i, step):
        return relay(held[i], y_relay_send.at[i, step], lax.rem(y + step, 4), z_hi)

    def onward(i, step):
        return relay(passed[i], onward_send.at[i, step], lax.rem(y + step, 4), z_hi)

    def to_partner():
        return pltpu.make_async_remote_copy(
            src_ref=p_own,
            dst_ref=p_row.at[col],
            send_sem=row_send.at[0],
            recv_sem=row_recv.at[col],
            device_id=(row, (1 - z_lo) * 8 + in_plane),
            device_id_type=MESH,
        )

    def to_row(half, step):
        which = lax.rem(z_lo + half, 2) * 8 + in_plane
        block = p_row.at[which]
        return pltpu.make_async_remote_copy(
            src_ref=block,
            dst_ref=block,
            send_sem=row_send.at[half * 4 + step],
            recv_sem=row_recv.at[which],
            device_id=(row, z_lo * 8 + lax.rem(in_plane + 2 * step, 8)),
            device_id_type=MESH,
        )

    def to_sibling(step):
        which = lax.rem(chip + step, 8) * 2 + core
        block = p_row.at[which]
        return pltpu.make_async_remote_copy(
            src_ref=block,
            dst_ref=block,
            send_sem=row_fwd.at[step],
            recv_sem=row_recv.at[which],
            device_id=(row, chip * 2 + 1 - core),
            device_id_type=MESH,
        )

    def row_arrived(which):
        pltpu.make_async_copy(p_own, p_row.at[which], row_recv.at[which]).wait()

    to_partner().start()
    to_sibling(0).start()
    for i in range(2):
        arrived(*held[i])
        for step in (1, 3):
            along_z(i, step).start()
        for step in (2, 1, 3):
            along_y(i, step).start()

    for step in (2, 1, 3):
        to_row(0, step).start()
    row_arrived((1 - z_lo) * 8 + in_plane)
    for step in (2, 1, 3):
        to_row(1, step).start()
    to_sibling(4).start()

    for i in range(2):
        arrived(*passed[i])
        for step in (1, 3):
            onward(i, step).start()

    for step in (1, 2, 3, 5, 6, 7):
        row_arrived(lax.rem(chip + step, 8) * 2 + core)
        to_sibling(step).start()

    for i in range(4):
        for step in (0, 1):
            row_arrived(4 * i + 2 * step + 1 - core)
        high, low = split(p_row[pl.ds(4 * i, 4)].reshape(256, 256))
        pt_high[:, pl.ds(256 * i, 256)] = high.T
        pt_low[:, pl.ds(256 * i, 256)] = low.T

    @pl.loop(0, 4)
    def _(j):
        high, low = split(dot3(pt_high[...], pt_low[...], t_high[j], t_low[j]))
        pt_t_high[j] = high
        pt_t_low[j] = low

    total = jnp.zeros((256, 256), F32)
    for step, rest in ((0, (1, 2)), (2, (0, 3)), (1, (0, 2, 1, 3)), (3, (0, 2, 1, 3))):
        quarter = lax.rem(y + step, 4)
        for i in rest:
            arrived(quarter, lax.rem(z_hi + i, 4))
        high, low = split(p_col[quarter])
        p_col_high[quarter] = high
        p_col_low[quarter] = low
        total += dot3(pt_t_high[quarter], pt_t_low[quarter], high, low)
    m_own[...] = m_own[...] - 2.0 * total.reshape(32, 8, 256)
    m_in[place] = m_own[place]

    def to_plane(step):
        which = lax.rem(place + step, 32)
        return pltpu.make_async_remote_copy(
            src_ref=m_own.at[which],
            dst_ref=m_in.at[place],
            send_sem=m_send.at[step],
            recv_sem=m_recv.at[place],
            device_id=in_plane_id(which),
            device_id_type=MESH,
        )

    @pl.loop(1, 32)
    def _(step):
        to_plane(step).start()

    @pl.loop(0, 4)
    def _(i):
        rows = pl.ds(pl.multiple_of(256 * i, 256), 256)
        total = jnp.zeros((256, 256), F32)
        for j in range(4):
            total += dot3(t_high[j, rows], t_low[j, rows], p_col_high[j], p_col_low[j])
        product[pl.ds(2 * i, 2)] = total.reshape(2, 2, 64, 256)

    to_pair = pltpu.make_async_remote_copy(
        src_ref=product.at[:, 1 - core],
        dst_ref=sibling,
        send_sem=sib_send,
        recv_sem=sib_recv,
        device_id=(row, chip * 2 + 1 - core),
        device_id_type=MESH,
    )
    to_pair.start()
    to_pair.wait_recv()
    for i in range(8):
        pair_sum[i] = product[i, core] + sibling[i]

    def to_chip(step):
        which = lax.rem(chip + step, 8)
        return pltpu.make_async_remote_copy(
            src_ref=pair_sum.at[which],
            dst_ref=pair_in.at[chip],
            send_sem=pair_send.at[step],
            recv_sem=pair_recv.at[chip],
            device_id=(row, which * 2 + core),
            device_id_type=MESH,
        )

    @pl.loop(1, 32)
    def _(step):
        which = lax.rem(place + step, 32)
        pltpu.make_async_copy(md_own, m_in.at[which], m_recv.at[which]).wait()

    total = m_in[0]
    for i in range(1, 32):
        total += m_in[i]
    m_sum[...] = total
    m_plane[z] = total

    def to_z(step):
        return pltpu.make_async_remote_copy(
            src_ref=m_sum,
            dst_ref=m_plane.at[z],
            send_sem=z_send.at[step],
            recv_sem=z_recv.at[z],
            device_id=z_id(lax.rem(z + step, 8)),
            device_id_type=MESH,
        )

    @pl.loop(1, 8)
    def _(step):
        to_z(step).start()

    @pl.loop(1, 8)
    def _(step):
        to_chip(step).start()

    @pl.loop(1, 8)
    def _(step):
        which = lax.rem(z + step, 8)
        pltpu.make_async_copy(md_own, m_plane.at[which], z_recv.at[which]).wait()

    total = m_plane[0]
    for i in range(1, 8):
        total += m_plane[i]
    high, low = split(jnp.concatenate([total, total], axis=0))
    total = dot3(high, low, d_high[...], d_low[...])[0:8]
    md_own[...] = total
    md[place] = total

    def to_all(step):
        return pltpu.make_async_remote_copy(
            src_ref=md_own,
            dst_ref=md.at[place],
            send_sem=out_send.at[step],
            recv_sem=out_recv.at[place],
            device_id=in_plane_id(lax.rem(place + step, 32)),
            device_id_type=MESH,
        )

    @pl.loop(1, 32)
    def _(step):
        to_all(step).start()

    @pl.loop(1, 8)
    def _(step):
        which = lax.rem(chip + step, 8)
        pltpu.make_async_copy(p_own, pair_in.at[which], pair_recv.at[which]).wait()

    reduced = pair_sum[chip]
    for step in range(1, 8):
        reduced += pair_in[lax.rem(chip + step, 8)]
    high, low = split(a_own[...] - 2.0 * reduced)
    solved_ref[...] = dot3(high, low, d_high[...], d_low[...])
    c_copy.wait()

    @pl.when(jnp.logical_not(diagonal))
    def _():
        spread(0).wait_send()

    spread(1).wait_send()
    for i in range(2):
        for step in (1, 2, 3):
            along_y(i, step).wait_send()
        for step in (1, 3):
            along_z(i, step).wait_send()
            onward(i, step).wait_send()
    to_sibling(0).wait_send()
    to_partner().wait_send()
    for step in (1, 2, 3):
        to_row(0, step).wait_send()
        to_row(1, step).wait_send()
    to_pair.wait_send()

    @pl.loop(1, 8)
    def _(step):
        to_sibling(step).wait_send()
        to_chip(step).wait_send()
        to_z(step).wait_send()

    @pl.loop(1, 32)
    def _(step):
        to_plane(step).wait_send()
        to_all(step).wait_send()

    @pl.loop(1, 32)
    def _(step):
        which = lax.rem(place + step, 32)
        pltpu.make_async_copy(md_own, md.at[which], out_recv.at[which]).wait()

    corner_ref[...] = c_raw[...] - md[...].reshape(256, 256).T


def body(*arrays):
    hbm = pl.BlockSpec(memory_space=pltpu.HBM)
    vmem = pl.BlockSpec(memory_space=pltpu.VMEM)
    dma = pltpu.SemaphoreType.DMA
    return pl.pallas_call(
        kernel,
        out_shape=(
            jax.ShapeDtypeStruct((64, 256), F32),
            jax.ShapeDtypeStruct((256, 256), F32),
        ),
        in_specs=[hbm] * 5,
        out_specs=(vmem, vmem),
        scratch_shapes=[
            pltpu.VMEM((1024, 1024), F32),
            pltpu.VMEM((4, 1024, 256), BF16),
            pltpu.VMEM((4, 1024, 256), BF16),
            pltpu.VMEM((64, 256), F32),
            pltpu.VMEM((64, 256), F32),
            pltpu.VMEM((256, 256), F32),
            pltpu.VMEM((256, 256), F32),
            pltpu.VMEM((256, 256), BF16),
            pltpu.VMEM((256, 256), BF16),
            pltpu.VMEM((4, 256, 256), F32),
            pltpu.VMEM((16, 64, 256), F32),
            pltpu.VMEM((256, 1024), BF16),
            pltpu.VMEM((256, 1024), BF16),
            pltpu.VMEM((4, 256, 256), BF16),
            pltpu.VMEM((4, 256, 256), BF16),
            pltpu.VMEM((4, 256, 256), BF16),
            pltpu.VMEM((4, 256, 256), BF16),
            pltpu.VMEM((8, 2, 64, 256), F32),
            pltpu.VMEM((8, 64, 256), F32),
            pltpu.VMEM((8, 64, 256), F32),
            pltpu.VMEM((8, 64, 256), F32),
            pltpu.VMEM((32, 8, 256), F32),
            pltpu.VMEM((32, 8, 256), F32),
            pltpu.VMEM((8, 256), F32),
            pltpu.VMEM((8, 8, 256), F32),
            pltpu.VMEM((8, 256), F32),
            pltpu.VMEM((32, 8, 256), F32),
            dma((8,)),
            dma((2,)),
            dma((4, 4)),
            dma((2, 4)),
            dma((2, 4)),
            dma((2, 4)),
            dma((8,)),
            dma((8,)),
            dma((16,)),
            dma(()),
            dma(()),
            dma((8,)),
            dma((8,)),
            dma((32,)),
            dma((32,)),
            dma((8,)),
            dma((8,)),
            dma((32,)),
            dma((32,)),
        ],
        compiler_params=pltpu.CompilerParams(
            collective_id=0, has_side_effects=True, vmem_limit_bytes=32 * 1024 * 1024
        ),
        name="adjoint_panel",
    )(*(pltpu.with_memory_space_constraint(x, pltpu.HBM) for x in arrays))


def solution(mesh):
    placed = (P("row", "col"), P(("row", "col"), None), P(("row", "col"), None), P(), P())
    return jax.shard_map(
        body, mesh=mesh, in_specs=placed, out_specs=(P(("row", "col"), None), P()), check_vma=False
    )
```

```python
import functools

import jax
import jax.numpy as jnp
from jax import lax
from jax.experimental import pallas as pl
from jax.experimental.pallas import tpu as pltpu
from jax.sharding import PartitionSpec as P

MESH = pl.DeviceIdType.MESH
F32 = jnp.float32
BF16 = jnp.bfloat16


def split(value):
    high = value.astype(BF16)
    return high, (value - high.astype(F32)).astype(BF16)


def dot3(a_high, a_low, b_high, b_low):
    dot = functools.partial(jnp.dot, preferred_element_type=F32)
    return dot(a_high, b_high) + (dot(a_high, b_low) + dot(a_low, b_high))


def kernel(
    t_hbm, p_hbm, a_hbm, d_hbm, c_hbm, solved_ref, corner_ref,
    t_raw, t_high, t_low, p_own, a_own, d_raw, c_raw, d_high, d_low,
    p_col, p_row, pt_high, pt_low, pt_t_high, pt_t_low, p_col_high, p_col_low, product,
    sibling, pair_sum, pair_in, x_sum, x_in, m_own, m_in, m_sum, m_plane, md_own, md,
    local_sem, spread_send, col_recv, z_relay_send, y_relay_send, onward_send,
    row_send, row_fwd, row_recv, sib_send, sib_recv, pair_send, pair_recv, other_send, other_recv,
    m_send, m_recv, z_send, z_recv, out_send, out_recv,
):
    row, col = lax.axis_index("row"), lax.axis_index("col")
    y, z_hi = row // 4, lax.rem(row, 4)
    z_lo, in_plane, core = col // 8, lax.rem(col, 8), lax.rem(col, 2)
    chip = col // 2
    z = z_hi * 2 + z_lo
    x, place = in_plane // 2, y * 8 + in_plane
    far_y, far_z, next_z, last_z = (
        lax.rem(y + 2, 4), lax.rem(z_hi + 2, 4), lax.rem(z_hi + 1, 4), lax.rem(z_hi + 3, 4)
    )

    def opposite(which):
        return lax.rem(which // 4 + 2, 4) * 4 + lax.rem(which + 2, 4)

    def in_plane_id(which):
        return ((which // 8) * 4 + z_hi, z_lo * 8 + lax.rem(which, 8))

    def z_id(which):
        return (y * 4 + which // 2, lax.rem(which, 2) * 8 + in_plane)

    slabs = [
        pltpu.make_async_copy(
            t_hbm.at[pl.ds(256 * i, 256)], t_raw.at[pl.ds(256 * i, 256)], local_sem.at[i]
        )
        for i in range(4)
    ]
    p_copy = pltpu.make_async_copy(p_hbm, p_own, local_sem.at[4])
    a_copy = pltpu.make_async_copy(a_hbm, a_own, local_sem.at[5])
    d_copy = pltpu.make_async_copy(d_hbm, d_raw, local_sem.at[6])
    c_copy = pltpu.make_async_copy(c_hbm, c_raw, local_sem.at[7])
    for copy in [p_copy, a_copy] + slabs + [d_copy, c_copy]:
        copy.start()

    barrier = pltpu.get_barrier_semaphore()

    def greet(device_id):
        pl.semaphore_signal(barrier, inc=1, device_id=device_id, device_id_type=MESH)

    diagonal = row == col

    @pl.when(jnp.logical_not(diagonal))
    def _():
        greet((col, row))

    greet((col, opposite(row)))

    @pl.loop(1, 8)
    def _(step):
        greet(z_id(lax.rem(z + step, 8)))

    @pl.loop(1, 32)
    def _(step):
        greet(in_plane_id(lax.rem(place + step, 32)))

    p_copy.wait()
    p_row[col] = p_own[...]
    pl.semaphore_wait(barrier, 2 + 7 + 31 - diagonal.astype(jnp.int32))

    def piece(quarter, which):
        return p_col.at[quarter, pl.ds(pl.multiple_of(64 * which, 64), 64)]

    def arrived(quarter, which):
        pltpu.make_async_copy(p_own, piece(quarter, which), col_recv.at[quarter, which]).wait()

    own_piece = piece(col // 4, lax.rem(col, 4))
    own_recv = col_recv.at[col // 4, lax.rem(col, 4)]

    def spread(i):
        return pltpu.make_async_remote_copy(
            src_ref=p_own,
            dst_ref=own_piece,
            send_sem=spread_send.at[i],
            recv_sem=own_recv,
            device_id=((col, opposite(col))[i], row),
            device_id_type=MESH,
        )

    @pl.when(diagonal)
    def _():
        pltpu.make_async_copy(p_own, own_piece, own_recv).start()

    @pl.when(jnp.logical_not(diagonal))
    def _():
        spread(0).start()

    spread(1).start()

    held = ((y, z_hi), (far_y, far_z))
    passed = ((y, last_z), (far_y, next_z))

    def relay(source, send_sem, to_y, to_z):
        return pltpu.make_async_remote_copy(
            src_ref=piece(*source),
            dst_ref=piece(*source),
            send_sem=send_sem,
            recv_sem=col_recv.at[source[0], source[1]],
            device_id=(to_y * 4 + to_z, col),
            device_id_type=MESH,
        )

    def along_z(i, step):
        return relay(held[i], z_relay_send.at[i, step], y, lax.rem(z_hi + step, 4))

    def along_y(i, step):
        return relay(held[i], y_relay_send.at[i, step], lax.rem(y + step, 4), z_hi)

    def onward(i, step):
        return relay(passed[i], onward_send.at[i, step], lax.rem(y + step, 4), z_hi)

    def to_partner():
        return pltpu.make_async_remote_copy(
            src_ref=p_own,
            dst_ref=p_row.at[col],
            send_sem=row_send.at[0],
            recv_sem=row_recv.at[col],
            device_id=(row, (1 - z_lo) * 8 + in_plane),
            device_id_type=MESH,
        )

    def to_row(half, step):
        which = lax.rem(z_lo + half, 2) * 8 + in_plane
        block = p_row.at[which]
        return pltpu.make_async_remote_copy(
            src_ref=block,
            dst_ref=block,
            send_sem=row_send.at[half * 4 + step],
            recv_sem=row_recv.at[which],
            device_id=(row, z_lo * 8 + lax.rem(in_plane + 2 * step, 8)),
            device_id_type=MESH,
        )

    def to_sibling(step):
        which = lax.rem(chip + step, 8) * 2 + core
        block = p_row.at[which]
        return pltpu.make_async_remote_copy(
            src_ref=block,
            dst_ref=block,
            send_sem=row_fwd.at[step],
            recv_sem=row_recv.at[which],
            device_id=(row, chip * 2 + 1 - core),
            device_id_type=MESH,
        )

    def row_arrived(which):
        pltpu.make_async_copy(p_own, p_row.at[which], row_recv.at[which]).wait()

    to_partner().start()
    to_sibling(0).start()

    a_copy.wait()
    p_high, p_low = split(p_own[...])
    a_high, a_low = split(a_own[...])
    m_own[...] = dot3(p_high.T, p_low.T, a_high, a_low).reshape(32, 8, 256)
    for i in range(4):
        slabs[i].wait()

        @pl.loop(0, 4)
        def _(j, i=i):
            rows = pl.ds(256 * i, 256)
            high, low = split(t_raw[rows, pl.ds(pl.multiple_of(256 * j, 256), 256)])
            t_high[j, rows] = high
            t_low[j, rows] = low

    d_copy.wait()
    high, low = split(d_raw[...])
    d_high[...] = high
    d_low[...] = low

    for step in (2, 1, 3):
        to_row(0, step).start()
    row_arrived((1 - z_lo) * 8 + in_plane)
    for step in (2, 1, 3):
        to_row(1, step).start()
    to_sibling(4).start()

    for i in range(2):
        arrived(*held[i])
        for step in (1, 3):
            along_z(i, step).start()
        for step in (2, 1, 3):
            along_y(i, step).start()

    for i in range(2):
        arrived(*passed[i])
        for step in (1, 3):
            onward(i, step).start()

    for step in (1, 2, 3, 5, 6, 7):
        row_arrived(lax.rem(chip + step, 8) * 2 + core)
        to_sibling(step).start()

    for i in range(4):
        for step in (0, 1):
            row_arrived(4 * i + 2 * step + 1 - core)
        high, low = split(p_row[pl.ds(4 * i, 4)].reshape(256, 256))
        pt_high[:, pl.ds(256 * i, 256)] = high.T
        pt_low[:, pl.ds(256 * i, 256)] = low.T

    @pl.loop(0, 4)
    def _(j):
        high, low = split(dot3(pt_high[...], pt_low[...], t_high[j], t_low[j]))
        pt_t_high[j] = high
        pt_t_low[j] = low

    total = jnp.zeros((256, 256), F32)
    for step, rest in ((0, (1, 2)), (2, (0, 3)), (1, (0, 2, 1, 3)), (3, (0, 2, 1, 3))):
        quarter = lax.rem(y + step, 4)
        for i in rest:
            arrived(quarter, lax.rem(z_hi + i, 4))
        high, low = split(p_col[quarter])
        p_col_high[quarter] = high
        p_col_low[quarter] = low
        total += dot3(pt_t_high[quarter], pt_t_low[quarter], high, low)
    m_own[...] = m_own[...] - 2.0 * total.reshape(32, 8, 256)
    m_in[place] = m_own[place]

    def to_plane(step):
        which = lax.rem(place + step, 32)
        return pltpu.make_async_remote_copy(
            src_ref=m_own.at[which],
            dst_ref=m_in.at[place],
            send_sem=m_send.at[step],
            recv_sem=m_recv.at[place],
            device_id=in_plane_id(which),
            device_id_type=MESH,
        )

    @pl.loop(1, 32)
    def _(step):
        to_plane(step).start()

    @pl.loop(0, 4)
    def _(i):
        rows = pl.ds(pl.multiple_of(256 * i, 256), 256)
        total = jnp.zeros((256, 256), F32)
        for j in range(4):
            total += dot3(t_high[j, rows], t_low[j, rows], p_col_high[j], p_col_low[j])
        product[pl.ds(2 * i, 2)] = total.reshape(2, 2, 64, 256)

    to_pair = pltpu.make_async_remote_copy(
        src_ref=product.at[:, 1 - core],
        dst_ref=sibling,
        send_sem=sib_send,
        recv_sem=sib_recv,
        device_id=(row, chip * 2 + 1 - core),
        device_id_type=MESH,
    )
    to_pair.start()
    to_pair.wait_recv()
    for i in range(8):
        pair_sum[i] = product[i, core] + sibling[i]

    def to_chip(step, half):
        return pltpu.make_async_remote_copy(
            src_ref=pair_sum.at[half * 4 + lax.rem(x + step, 4)],
            dst_ref=pair_in.at[half * 4 + x],
            send_sem=pair_send.at[half * 4 + step],
            recv_sem=pair_recv.at[half * 4 + x],
            device_id=(row, z_lo * 8 + lax.rem(in_plane + 2 * step, 8)),
            device_id_type=MESH,
        )

    for half in range(2):
        for step in (2, 1, 3):
            to_chip(step, half).start()

    @pl.loop(1, 32)
    def _(step):
        which = lax.rem(place + step, 32)
        pltpu.make_async_copy(md_own, m_in.at[which], m_recv.at[which]).wait()

    total = m_in[0]
    for i in range(1, 32):
        total += m_in[i]
    m_sum[...] = total
    m_plane[z] = total

    def to_z(step):
        return pltpu.make_async_remote_copy(
            src_ref=m_sum,
            dst_ref=m_plane.at[z],
            send_sem=z_send.at[step],
            recv_sem=z_recv.at[z],
            device_id=z_id(lax.rem(z + step, 8)),
            device_id_type=MESH,
        )

    @pl.loop(1, 8)
    def _(step):
        to_z(step).start()

    @pl.loop(1, 8)
    def _(step):
        which = lax.rem(z + step, 8)
        pltpu.make_async_copy(md_own, m_plane.at[which], z_recv.at[which]).wait()

    total = m_plane[0]
    for i in range(1, 8):
        total += m_plane[i]
    high, low = split(jnp.concatenate([total, total], axis=0))
    total = dot3(high, low, d_high[...], d_low[...])[0:8]
    md_own[...] = total
    md[place] = total

    def to_all(step):
        return pltpu.make_async_remote_copy(
            src_ref=md_own,
            dst_ref=md.at[place],
            send_sem=out_send.at[step],
            recv_sem=out_recv.at[place],
            device_id=in_plane_id(lax.rem(place + step, 32)),
            device_id_type=MESH,
        )

    @pl.loop(1, 32)
    def _(step):
        to_all(step).start()

    for half in range(2):
        for step in (1, 2, 3):
            which = half * 4 + lax.rem(x + step, 4)
            pltpu.make_async_copy(p_own, pair_in.at[which], pair_recv.at[which]).wait()
        reduced = pair_sum[half * 4 + x]
        for step in (1, 2, 3):
            reduced += pair_in[half * 4 + lax.rem(x + step, 4)]
        x_sum[half] = reduced

    to_other = pltpu.make_async_remote_copy(
        src_ref=x_sum.at[1 - z_lo],
        dst_ref=x_in,
        send_sem=other_send,
        recv_sem=other_recv,
        device_id=(row, (1 - z_lo) * 8 + in_plane),
        device_id_type=MESH,
    )
    to_other.start()
    to_other.wait_recv()
    reduced = x_sum[z_lo] + x_in[...]
    high, low = split(a_own[...] - 2.0 * reduced)
    solved_ref[...] = dot3(high, low, d_high[...], d_low[...])
    c_copy.wait()

    @pl.when(jnp.logical_not(diagonal))
    def _():
        spread(0).wait_send()

    spread(1).wait_send()
    for i in range(2):
        for step in (1, 2, 3):
            along_y(i, step).wait_send()
        for step in (1, 3):
            along_z(i, step).wait_send()
            onward(i, step).wait_send()
    to_sibling(0).wait_send()
    to_partner().wait_send()
    for step in (1, 2, 3):
        to_row(0, step).wait_send()
        to_row(1, step).wait_send()
    to_pair.wait_send()
    to_other.wait_send()
    for step in (1, 2, 3):
        to_chip(step, 0).wait_send()
        to_chip(step, 1).wait_send()

    @pl.loop(1, 8)
    def _(step):
        to_sibling(step).wait_send()
        to_z(step).wait_send()

    @pl.loop(1, 32)
    def _(step):
        to_plane(step).wait_send()
        to_all(step).wait_send()

    @pl.loop(1, 32)
    def _(step):
        which = lax.rem(place + step, 32)
        pltpu.make_async_copy(md_own, md.at[which], out_recv.at[which]).wait()

    corner_ref[...] = c_raw[...] - md[...].reshape(256, 256).T


def body(*arrays):
    hbm = pl.BlockSpec(memory_space=pltpu.HBM)
    vmem = pl.BlockSpec(memory_space=pltpu.VMEM)
    dma = pltpu.SemaphoreType.DMA
    return pl.pallas_call(
        kernel,
        out_shape=(
            jax.ShapeDtypeStruct((64, 256), F32),
            jax.ShapeDtypeStruct((256, 256), F32),
        ),
        in_specs=[hbm] * 5,
        out_specs=(vmem, vmem),
        scratch_shapes=[
            pltpu.VMEM((1024, 1024), F32),
            pltpu.VMEM((4, 1024, 256), BF16),
            pltpu.VMEM((4, 1024, 256), BF16),
            pltpu.VMEM((64, 256), F32),
            pltpu.VMEM((64, 256), F32),
            pltpu.VMEM((256, 256), F32),
            pltpu.VMEM((256, 256), F32),
            pltpu.VMEM((256, 256), BF16),
            pltpu.VMEM((256, 256), BF16),
            pltpu.VMEM((4, 256, 256), F32),
            pltpu.VMEM((16, 64, 256), F32),
            pltpu.VMEM((256, 1024), BF16),
            pltpu.VMEM((256, 1024), BF16),
            pltpu.VMEM((4, 256, 256), BF16),
            pltpu.VMEM((4, 256, 256), BF16),
            pltpu.VMEM((4, 256, 256), BF16),
            pltpu.VMEM((4, 256, 256), BF16),
            pltpu.VMEM((8, 2, 64, 256), F32),
            pltpu.VMEM((8, 64, 256), F32),
            pltpu.VMEM((8, 64, 256), F32),
            pltpu.VMEM((8, 64, 256), F32),
            pltpu.VMEM((2, 64, 256), F32),
            pltpu.VMEM((64, 256), F32),
            pltpu.VMEM((32, 8, 256), F32),
            pltpu.VMEM((32, 8, 256), F32),
            pltpu.VMEM((8, 256), F32),
            pltpu.VMEM((8, 8, 256), F32),
            pltpu.VMEM((8, 256), F32),
            pltpu.VMEM((32, 8, 256), F32),
            dma((8,)),
            dma((2,)),
            dma((4, 4)),
            dma((2, 4)),
            dma((2, 4)),
            dma((2, 4)),
            dma((8,)),
            dma((8,)),
            dma((16,)),
            dma(()),
            dma(()),
            dma((8,)),
            dma((8,)),
            dma(()),
            dma(()),
            dma((32,)),
            dma((32,)),
            dma((8,)),
            dma((8,)),
            dma((32,)),
            dma((32,)),
        ],
        compiler_params=pltpu.CompilerParams(
            collective_id=0, has_side_effects=True, vmem_limit_bytes=32 * 1024 * 1024
        ),
        name="adjoint_panel",
    )(*(pltpu.with_memory_space_constraint(x, pltpu.HBM) for x in arrays))


def solution(mesh):
    placed = (P("row", "col"), P(("row", "col"), None), P(("row", "col"), None), P(), P())
    return jax.shard_map(
        body, mesh=mesh, in_specs=placed, out_specs=(P(("row", "col"), None), P()), check_vma=False
    )
```

```python
import functools

import jax
import jax.numpy as jnp
from jax import lax
from jax.experimental import pallas as pl
from jax.experimental.pallas import tpu as pltpu
from jax.sharding import PartitionSpec as P

MESH = pl.DeviceIdType.MESH
F32 = jnp.float32
BF16 = jnp.bfloat16


def split(value):
    high = value.astype(BF16)
    return high, (value - high.astype(F32)).astype(BF16)


def dot3(a_high, a_low, b_high, b_low):
    dot = functools.partial(jnp.dot, preferred_element_type=F32)
    return dot(a_high, b_high) + (dot(a_high, b_low) + dot(a_low, b_high))


def kernel(
    t_hbm, p_hbm, a_hbm, d_hbm, c_hbm, solved_ref, corner_ref,
    t_raw, t_high, t_low, p_own, a_own, d_raw, c_raw, d_high, d_low,
    p_col, p_row, pt_high, pt_low, pt_t_high, pt_t_low, p_col_high, p_col_low, product,
    sibling, pair_sum, pair_in, x_sum, x_in, m_own, m_in, m_sum, m_plane, md_own, md,
    local_sem, spread_send, col_recv, z_relay_send, y_relay_send, onward_send,
    row_send, row_fwd, row_recv, sib_send, sib_recv, pair_send, pair_recv, other_send, other_recv,
    m_send, m_recv, z_send, z_recv, out_send, out_recv,
):
    row, col = lax.axis_index("row"), lax.axis_index("col")
    y, z_hi = lax.div(row, 4), lax.rem(row, 4)
    z_lo, in_plane, core = lax.div(col, 8), lax.rem(col, 8), lax.rem(col, 2)
    chip = lax.div(col, 2)
    z = z_hi * 2 + z_lo
    x, place = lax.div(in_plane, 2), y * 8 + in_plane
    far_y, far_z, next_z, last_z = (
        lax.rem(y + 2, 4), lax.rem(z_hi + 2, 4), lax.rem(z_hi + 1, 4), lax.rem(z_hi + 3, 4)
    )

    def opposite(which):
        return lax.rem(lax.div(which, 4) + 2, 4) * 4 + lax.rem(which + 2, 4)

    rows = [lax.rem(y + step, 4) for step in range(4)]
    places = [lax.rem(in_plane + step, 8) for step in range(8)]
    plane = [
        (rows[i] * 8 + places[j], (rows[i] * 4 + z_hi, z_lo * 8 + places[j]))
        for i in (2, 1, 3, 0)
        for j in (4, 5, 3, 2, 6, 1, 7, 0)
        if i or j
    ]
    along_z_ids = []
    for step in (4, 3, 5, 2, 6, 1, 7):
        to_z = lax.rem(z + step, 8)
        along_z_ids.append((y * 4 + lax.div(to_z, 2), lax.rem(to_z, 2) * 8 + in_plane))

    def whole(pieces, count, sem):
        pltpu.make_async_copy(
            pieces.at[pl.ds(0, count)], pieces.at[pl.ds(0, count)], sem
        ).wait()

    slabs = [
        pltpu.make_async_copy(
            t_hbm.at[pl.ds(256 * i, 256)], t_raw.at[pl.ds(256 * i, 256)], local_sem.at[i]
        )
        for i in range(4)
    ]
    p_copy = pltpu.make_async_copy(p_hbm, p_own, local_sem.at[4])
    a_copy = pltpu.make_async_copy(a_hbm, a_own, local_sem.at[5])
    d_copy = pltpu.make_async_copy(d_hbm, d_raw, local_sem.at[6])
    c_copy = pltpu.make_async_copy(c_hbm, c_raw, local_sem.at[7])
    for copy in [p_copy, a_copy] + slabs + [d_copy, c_copy]:
        copy.start()

    barrier = pltpu.get_barrier_semaphore()

    def greet(device_id):
        pl.semaphore_signal(barrier, inc=1, device_id=device_id, device_id_type=MESH)

    diagonal = row == col

    @pl.when(jnp.logical_not(diagonal))
    def _():
        greet((col, row))

    greet((col, opposite(row)))

    for device_id in along_z_ids:
        greet(device_id)

    for _, device_id in plane:
        greet(device_id)

    p_copy.wait()
    p_row[col] = p_own[...]
    pl.semaphore_wait(barrier, 2 + 7 + 31 - diagonal.astype(jnp.int32))

    def piece(quarter, which):
        return p_col.at[quarter, pl.ds(pl.multiple_of(64 * which, 64), 64)]

    def arrived(quarter, which):
        pltpu.make_async_copy(p_own, piece(quarter, which), col_recv.at[quarter, which]).wait()

    own_piece = piece(lax.div(col, 4), lax.rem(col, 4))
    own_recv = col_recv.at[lax.div(col, 4), lax.rem(col, 4)]

    def spread(i):
        return pltpu.make_async_remote_copy(
            src_ref=p_own,
            dst_ref=own_piece,
            send_sem=spread_send.at[i],
            recv_sem=own_recv,
            device_id=((col, opposite(col))[i], row),
            device_id_type=MESH,
        )

    @pl.when(diagonal)
    def _():
        pltpu.make_async_copy(p_own, own_piece, own_recv).start()

    @pl.when(jnp.logical_not(diagonal))
    def _():
        spread(0).start()

    spread(1).start()

    held = ((y, z_hi), (far_y, far_z))
    passed = ((y, last_z), (far_y, next_z))

    def relay(source, send_sem, to_y, to_z):
        return pltpu.make_async_remote_copy(
            src_ref=piece(*source),
            dst_ref=piece(*source),
            send_sem=send_sem,
            recv_sem=col_recv.at[source[0], source[1]],
            device_id=(to_y * 4 + to_z, col),
            device_id_type=MESH,
        )

    def along_z(i, step):
        return relay(held[i], z_relay_send.at[i, step], y, lax.rem(z_hi + step, 4))

    def along_y(i, step):
        return relay(held[i], y_relay_send.at[i, step], lax.rem(y + step, 4), z_hi)

    def onward(i, step):
        return relay(passed[i], onward_send.at[i, step], lax.rem(y + step, 4), z_hi)

    def to_partner():
        return pltpu.make_async_remote_copy(
            src_ref=p_own,
            dst_ref=p_row.at[col],
            send_sem=row_send.at[0],
            recv_sem=row_recv.at[col],
            device_id=(row, (1 - z_lo) * 8 + in_plane),
            device_id_type=MESH,
        )

    def to_row(half, step):
        which = lax.rem(z_lo + half, 2) * 8 + in_plane
        block = p_row.at[which]
        return pltpu.make_async_remote_copy(
            src_ref=block,
            dst_ref=block,
            send_sem=row_send.at[half * 4 + step],
            recv_sem=row_recv.at[which],
            device_id=(row, z_lo * 8 + lax.rem(in_plane + 2 * step, 8)),
            device_id_type=MESH,
        )

    def to_sibling(step):
        which = lax.rem(chip + step, 8) * 2 + core
        block = p_row.at[which]
        return pltpu.make_async_remote_copy(
            src_ref=block,
            dst_ref=block,
            send_sem=row_fwd.at[step],
            recv_sem=row_recv.at[which],
            device_id=(row, chip * 2 + 1 - core),
            device_id_type=MESH,
        )

    def row_arrived(which):
        pltpu.make_async_copy(p_own, p_row.at[which], row_recv.at[which]).wait()

    to_partner().start()
    to_sibling(0).start()

    a_copy.wait()
    p_high, p_low = split(p_own[...])
    a_high, a_low = split(a_own[...])
    m_own[...] = dot3(p_high.T, p_low.T, a_high, a_low).reshape(32, 8, 256)
    for i in range(4):
        slabs[i].wait()

        @pl.loop(0, 4)
        def _(j, i=i):
            rows = pl.ds(256 * i, 256)
            high, low = split(t_raw[rows, pl.ds(pl.multiple_of(256 * j, 256), 256)])
            t_high[j, rows] = high
            t_low[j, rows] = low

    d_copy.wait()
    high, low = split(d_raw[...])
    d_high[...] = high
    d_low[...] = low

    for step in (2, 1, 3):
        to_row(0, step).start()
    row_arrived((1 - z_lo) * 8 + in_plane)
    for step in (2, 1, 3):
        to_row(1, step).start()
    to_sibling(4).start()

    for i in range(2):
        arrived(*held[i])
        for step in (1, 3):
            along_z(i, step).start()
        for step in (2, 1, 3):
            along_y(i, step).start()

    for i in range(2):
        arrived(*passed[i])
        for step in (1, 3):
            onward(i, step).start()

    for step in (1, 2, 3, 5, 6, 7):
        row_arrived(lax.rem(chip + step, 8) * 2 + core)
        to_sibling(step).start()

    for i in range(4):
        for step in (0, 1):
            row_arrived(4 * i + 2 * step + 1 - core)
        high, low = split(p_row[pl.ds(4 * i, 4)].reshape(256, 256))
        pt_high[:, pl.ds(256 * i, 256)] = high.T
        pt_low[:, pl.ds(256 * i, 256)] = low.T

    @pl.loop(0, 4)
    def _(j):
        high, low = split(dot3(pt_high[...], pt_low[...], t_high[j], t_low[j]))
        pt_t_high[j] = high
        pt_t_low[j] = low

    total = jnp.zeros((256, 256), F32)
    for step, rest in ((0, (1, 2)), (2, (0, 3)), (1, (0, 2, 1, 3)), (3, (0, 2, 1, 3))):
        quarter = lax.rem(y + step, 4)
        for i in rest:
            arrived(quarter, lax.rem(z_hi + i, 4))
        high, low = split(p_col[quarter])
        p_col_high[quarter] = high
        p_col_low[quarter] = low
        total += dot3(pt_t_high[quarter], pt_t_low[quarter], high, low)
    m_own[...] = m_own[...] - 2.0 * total.reshape(32, 8, 256)
    m_in[place] = m_own[place]

    for which, device_id in plane:
        pltpu.make_async_remote_copy(
            src_ref=m_own.at[which],
            dst_ref=m_in.at[place],
            send_sem=m_send,
            recv_sem=m_recv,
            device_id=device_id,
            device_id_type=MESH,
        ).start()

    @pl.loop(0, 4)
    def _(i):
        rows = pl.ds(pl.multiple_of(256 * i, 256), 256)
        total = jnp.zeros((256, 256), F32)
        for j in range(4):
            total += dot3(t_high[j, rows], t_low[j, rows], p_col_high[j], p_col_low[j])
        product[pl.ds(2 * i, 2)] = total.reshape(2, 2, 64, 256)

    to_pair = pltpu.make_async_remote_copy(
        src_ref=product.at[:, 1 - core],
        dst_ref=sibling,
        send_sem=sib_send,
        recv_sem=sib_recv,
        device_id=(row, chip * 2 + 1 - core),
        device_id_type=MESH,
    )
    to_pair.start()
    to_pair.wait_recv()
    for i in range(8):
        pair_sum[i] = product[i, core] + sibling[i]

    def to_chip(step, half):
        return pltpu.make_async_remote_copy(
            src_ref=pair_sum.at[half * 4 + lax.rem(x + step, 4)],
            dst_ref=pair_in.at[half * 4 + x],
            send_sem=pair_send.at[half * 4 + step],
            recv_sem=pair_recv.at[half * 4 + x],
            device_id=(row, z_lo * 8 + lax.rem(in_plane + 2 * step, 8)),
            device_id_type=MESH,
        )

    for half in range(2):
        for step in (2, 1, 3):
            to_chip(step, half).start()

    whole(m_in, 31, m_recv)

    total = m_in[0]
    for i in range(1, 32):
        total += m_in[i]
    m_sum[...] = total
    m_plane[z] = total

    for device_id in along_z_ids:
        pltpu.make_async_remote_copy(
            src_ref=m_sum,
            dst_ref=m_plane.at[z],
            send_sem=z_send,
            recv_sem=z_recv,
            device_id=device_id,
            device_id_type=MESH,
        ).start()

    whole(m_plane, 7, z_recv)

    total = m_plane[0]
    for i in range(1, 8):
        total += m_plane[i]
    high, low = split(jnp.concatenate([total, total], axis=0))
    total = dot3(high, low, d_high[...], d_low[...])[0:8]
    md_own[...] = total
    md[place] = total

    for _, device_id in plane:
        pltpu.make_async_remote_copy(
            src_ref=md_own,
            dst_ref=md.at[place],
            send_sem=out_send,
            recv_sem=out_recv,
            device_id=device_id,
            device_id_type=MESH,
        ).start()

    for half in range(2):
        for step in (1, 2, 3):
            which = half * 4 + lax.rem(x + step, 4)
            pltpu.make_async_copy(p_own, pair_in.at[which], pair_recv.at[which]).wait()
        reduced = pair_sum[half * 4 + x]
        for step in (1, 2, 3):
            reduced += pair_in[half * 4 + lax.rem(x + step, 4)]
        x_sum[half] = reduced

    to_other = pltpu.make_async_remote_copy(
        src_ref=x_sum.at[1 - z_lo],
        dst_ref=x_in,
        send_sem=other_send,
        recv_sem=other_recv,
        device_id=(row, (1 - z_lo) * 8 + in_plane),
        device_id_type=MESH,
    )
    to_other.start()
    to_other.wait_recv()
    reduced = x_sum[z_lo] + x_in[...]
    high, low = split(a_own[...] - 2.0 * reduced)
    solved_ref[...] = dot3(high, low, d_high[...], d_low[...])
    c_copy.wait()

    @pl.when(jnp.logical_not(diagonal))
    def _():
        spread(0).wait_send()

    spread(1).wait_send()
    for i in range(2):
        for step in (1, 2, 3):
            along_y(i, step).wait_send()
        for step in (1, 3):
            along_z(i, step).wait_send()
            onward(i, step).wait_send()
    to_sibling(0).wait_send()
    to_partner().wait_send()
    for step in (1, 2, 3):
        to_row(0, step).wait_send()
        to_row(1, step).wait_send()
    to_pair.wait_send()
    to_other.wait_send()
    for step in (1, 2, 3):
        to_chip(step, 0).wait_send()
        to_chip(step, 1).wait_send()

    @pl.loop(1, 8)
    def _(step):
        to_sibling(step).wait_send()

    whole(m_in, 31, m_send)
    whole(m_plane, 7, z_send)
    whole(md, 31, out_send)

    whole(md, 31, out_recv)

    corner_ref[...] = c_raw[...] - md[...].reshape(256, 256).T


def body(*arrays):
    hbm = pl.BlockSpec(memory_space=pltpu.HBM)
    vmem = pl.BlockSpec(memory_space=pltpu.VMEM)
    dma = pltpu.SemaphoreType.DMA
    return pl.pallas_call(
        kernel,
        out_shape=(
            jax.ShapeDtypeStruct((64, 256), F32),
            jax.ShapeDtypeStruct((256, 256), F32),
        ),
        in_specs=[hbm] * 5,
        out_specs=(vmem, vmem),
        scratch_shapes=[
            pltpu.VMEM((1024, 1024), F32),
            pltpu.VMEM((4, 1024, 256), BF16),
            pltpu.VMEM((4, 1024, 256), BF16),
            pltpu.VMEM((64, 256), F32),
            pltpu.VMEM((64, 256), F32),
            pltpu.VMEM((256, 256), F32),
            pltpu.VMEM((256, 256), F32),
            pltpu.VMEM((256, 256), BF16),
            pltpu.VMEM((256, 256), BF16),
            pltpu.VMEM((4, 256, 256), F32),
            pltpu.VMEM((16, 64, 256), F32),
            pltpu.VMEM((256, 1024), BF16),
            pltpu.VMEM((256, 1024), BF16),
            pltpu.VMEM((4, 256, 256), BF16),
            pltpu.VMEM((4, 256, 256), BF16),
            pltpu.VMEM((4, 256, 256), BF16),
            pltpu.VMEM((4, 256, 256), BF16),
            pltpu.VMEM((8, 2, 64, 256), F32),
            pltpu.VMEM((8, 64, 256), F32),
            pltpu.VMEM((8, 64, 256), F32),
            pltpu.VMEM((8, 64, 256), F32),
            pltpu.VMEM((2, 64, 256), F32),
            pltpu.VMEM((64, 256), F32),
            pltpu.VMEM((32, 8, 256), F32),
            pltpu.VMEM((32, 8, 256), F32),
            pltpu.VMEM((8, 256), F32),
            pltpu.VMEM((8, 8, 256), F32),
            pltpu.VMEM((8, 256), F32),
            pltpu.VMEM((32, 8, 256), F32),
            dma((8,)),
            dma((2,)),
            dma((4, 4)),
            dma((2, 4)),
            dma((2, 4)),
            dma((2, 4)),
            dma((8,)),
            dma((8,)),
            dma((16,)),
            dma(()),
            dma(()),
            dma((8,)),
            dma((8,)),
            dma(()),
            dma(()),
            dma(()),
            dma(()),
            dma(()),
            dma(()),
            dma(()),
            dma(()),
        ],
        compiler_params=pltpu.CompilerParams(
            collective_id=0, has_side_effects=True, vmem_limit_bytes=32 * 1024 * 1024
        ),
        name="adjoint_panel",
    )(*(pltpu.with_memory_space_constraint(x, pltpu.HBM) for x in arrays))


def solution(mesh):
    placed = (P("row", "col"), P(("row", "col"), None), P(("row", "col"), None), P(), P())
    return jax.shard_map(
        body, mesh=mesh, in_specs=placed, out_specs=(P(("row", "col"), None), P()), check_vma=False
    )
```

```python
import functools

import jax
import jax.numpy as jnp
from jax import lax
from jax.experimental import pallas as pl
from jax.experimental.pallas import tpu as pltpu
from jax.sharding import PartitionSpec as P

MESH = pl.DeviceIdType.MESH
F32 = jnp.float32
BF16 = jnp.bfloat16


def split(value):
    high = value.astype(BF16)
    return high, (value - high.astype(F32)).astype(BF16)


def dot3(a_high, a_low, b_high, b_low):
    dot = functools.partial(jnp.dot, preferred_element_type=F32)
    return dot(a_high, b_high) + (dot(a_high, b_low) + dot(a_low, b_high))


def kernel(
    t_hbm, p_hbm, a_hbm, d_hbm, c_hbm, solved_ref, corner_ref,
    t_raw, t_high, t_low, p_own, a_own, d_raw, c_raw, d_high, d_low,
    p_col, p_row, pt_high, pt_low, pt_t_high, pt_t_low, p_col_high, p_col_low, product,
    sibling, pair_sum, pair_in, x_sum, x_in, m_own, m_in, m_sum, m_plane, md_own, md,
    local_sem, spread_send, col_recv, z_relay_send, y_relay_send, onward_send, across_send,
    row_send, row_fwd, row_recv, sib_send, sib_recv, pair_send, pair_recv, other_send, other_recv,
    m_send, m_recv, z_send, z_recv, out_send, out_recv,
):
    row, col = lax.axis_index("row"), lax.axis_index("col")
    y, z_hi = lax.div(row, 4), lax.rem(row, 4)
    z_lo, in_plane, core = lax.div(col, 8), lax.rem(col, 8), lax.rem(col, 2)
    chip = lax.div(col, 2)
    z = z_hi * 2 + z_lo
    x, place = lax.div(in_plane, 2), y * 8 + in_plane
    far_y, far_z, next_z, last_z = (
        lax.rem(y + 2, 4), lax.rem(z_hi + 2, 4), lax.rem(z_hi + 1, 4), lax.rem(z_hi + 3, 4)
    )

    def opposite(which):
        return lax.rem(lax.div(which, 4) + 2, 4) * 4 + lax.rem(which + 2, 4)

    rows = [lax.rem(y + step, 4) for step in range(4)]
    places = [lax.rem(in_plane + step, 8) for step in range(8)]
    plane = [
        (rows[i] * 8 + places[j], (rows[i] * 4 + z_hi, z_lo * 8 + places[j]))
        for i in (2, 1, 3, 0)
        for j in (4, 5, 3, 2, 6, 1, 7, 0)
        if i or j
    ]
    along_z_ids = []
    for step in (4, 3, 5, 2, 6, 1, 7):
        to_z = lax.rem(z + step, 8)
        along_z_ids.append((y * 4 + lax.div(to_z, 2), lax.rem(to_z, 2) * 8 + in_plane))

    def whole(pieces, count, sem):
        pltpu.make_async_copy(
            pieces.at[pl.ds(0, count)], pieces.at[pl.ds(0, count)], sem
        ).wait()

    slabs = [
        pltpu.make_async_copy(
            t_hbm.at[pl.ds(256 * i, 256)], t_raw.at[pl.ds(256 * i, 256)], local_sem.at[i]
        )
        for i in range(4)
    ]
    p_copy = pltpu.make_async_copy(p_hbm, p_own, local_sem.at[4])
    a_copy = pltpu.make_async_copy(a_hbm, a_own, local_sem.at[5])
    d_copy = pltpu.make_async_copy(d_hbm, d_raw, local_sem.at[6])
    c_copy = pltpu.make_async_copy(c_hbm, c_raw, local_sem.at[7])
    for copy in [p_copy, a_copy] + slabs + [d_copy, c_copy]:
        copy.start()

    barrier = pltpu.get_barrier_semaphore()

    def greet(device_id):
        pl.semaphore_signal(barrier, inc=1, device_id=device_id, device_id_type=MESH)

    diagonal = row == col

    @pl.when(jnp.logical_not(diagonal))
    def _():
        greet((col, row))

    greet((col, opposite(row)))

    for device_id in along_z_ids:
        greet(device_id)

    for _, device_id in plane:
        greet(device_id)

    p_copy.wait()
    p_row[col] = p_own[...]
    def split_slab(i):
        slabs[i].wait()

        @pl.loop(0, 4)
        def _(j):
            rows = pl.ds(256 * i, 256)
            high, low = split(t_raw[rows, pl.ds(pl.multiple_of(256 * j, 256), 256)])
            t_high[j, rows] = high
            t_low[j, rows] = low

    split_slab(0)
    split_slab(1)

    pl.semaphore_wait(barrier, 2 + 7 + 31 - diagonal.astype(jnp.int32))

    def piece(quarter, which):
        return p_col.at[quarter, pl.ds(pl.multiple_of(64 * which, 64), 64)]

    def arrived(quarter, which):
        pltpu.make_async_copy(p_own, piece(quarter, which), col_recv.at[quarter, which]).wait()

    own_piece = piece(lax.div(col, 4), lax.rem(col, 4))
    own_recv = col_recv.at[lax.div(col, 4), lax.rem(col, 4)]

    def spread(i):
        return pltpu.make_async_remote_copy(
            src_ref=p_own,
            dst_ref=own_piece,
            send_sem=spread_send.at[i],
            recv_sem=own_recv,
            device_id=((col, opposite(col))[i], row),
            device_id_type=MESH,
        )

    @pl.when(diagonal)
    def _():
        pltpu.make_async_copy(p_own, own_piece, own_recv).start()

    @pl.when(jnp.logical_not(diagonal))
    def _():
        spread(0).start()

    spread(1).start()

    held = ((y, z_hi), (far_y, far_z))
    passed = ((y, last_z), (far_y, next_z))
    beside = ((rows[3], z_hi), (rows[3], far_z))

    def relay(source, send_sem, to_y, to_z):
        return pltpu.make_async_remote_copy(
            src_ref=piece(*source),
            dst_ref=piece(*source),
            send_sem=send_sem,
            recv_sem=col_recv.at[source[0], source[1]],
            device_id=(to_y * 4 + to_z, col),
            device_id_type=MESH,
        )

    def along_z(i, step):
        return relay(held[i], z_relay_send.at[i, step], y, lax.rem(z_hi + step, 4))

    def along_y(i, step):
        return relay(held[i], y_relay_send.at[i, step], lax.rem(y + step, 4), z_hi)

    def across(i):
        return relay(beside[i], across_send.at[i], lax.rem(y + 1 + 2 * i, 4), z_hi)

    def onward(i, step):
        return relay(passed[i], onward_send.at[i, step], lax.rem(y + step, 4), z_hi)

    def to_partner():
        return pltpu.make_async_remote_copy(
            src_ref=p_own,
            dst_ref=p_row.at[col],
            send_sem=row_send.at[0],
            recv_sem=row_recv.at[col],
            device_id=(row, (1 - z_lo) * 8 + in_plane),
            device_id_type=MESH,
        )

    def to_row(half, step):
        which = lax.rem(z_lo + half, 2) * 8 + in_plane
        block = p_row.at[which]
        return pltpu.make_async_remote_copy(
            src_ref=block,
            dst_ref=block,
            send_sem=row_send.at[half * 4 + step],
            recv_sem=row_recv.at[which],
            device_id=(row, z_lo * 8 + lax.rem(in_plane + 2 * step, 8)),
            device_id_type=MESH,
        )

    def to_sibling(step):
        which = lax.rem(chip + step, 8) * 2 + core
        block = p_row.at[which]
        return pltpu.make_async_remote_copy(
            src_ref=block,
            dst_ref=block,
            send_sem=row_fwd.at[step],
            recv_sem=row_recv.at[which],
            device_id=(row, chip * 2 + 1 - core),
            device_id_type=MESH,
        )

    def row_arrived(which):
        pltpu.make_async_copy(p_own, p_row.at[which], row_recv.at[which]).wait()

    to_partner().start()
    to_sibling(0).start()

    split_slab(2)
    split_slab(3)

    for step in (2, 1, 3):
        to_row(0, step).start()
    row_arrived((1 - z_lo) * 8 + in_plane)
    for step in (2, 1, 3):
        to_row(1, step).start()
    to_sibling(4).start()

    for i in range(2):
        arrived(*held[i])
        for step in (1, 3):
            along_z(i, step).start()
        for step in (1, 3):
            along_y(i, step).start()

    for i in range(2):
        arrived(*beside[i])
        across(i).start()

    for i in range(2):
        arrived(*passed[i])
        for step in (1, 3):
            onward(i, step).start()

    a_copy.wait()
    p_high, p_low = split(p_own[...])
    a_high, a_low = split(a_own[...])
    m_own[...] = dot3(p_high.T, p_low.T, a_high, a_low).reshape(32, 8, 256)

    for step in (1, 2, 3, 5, 6, 7):
        row_arrived(lax.rem(chip + step, 8) * 2 + core)
        to_sibling(step).start()

    for i in range(4):
        for step in (0, 1):
            row_arrived(4 * i + 2 * step + 1 - core)
        high, low = split(p_row[pl.ds(4 * i, 4)].reshape(256, 256))
        pt_high[:, pl.ds(256 * i, 256)] = high.T
        pt_low[:, pl.ds(256 * i, 256)] = low.T

    @pl.loop(0, 4)
    def _(j):
        high, low = split(dot3(pt_high[...], pt_low[...], t_high[j], t_low[j]))
        pt_t_high[j] = high
        pt_t_low[j] = low

    total = jnp.zeros((256, 256), F32)
    for step, rest in ((0, (1, 2)), (2, (0, 3)), (1, (0, 2, 1, 3)), (3, (1, 3))):
        quarter = lax.rem(y + step, 4)
        for i in rest:
            arrived(quarter, lax.rem(z_hi + i, 4))
        high, low = split(p_col[quarter])
        p_col_high[quarter] = high
        p_col_low[quarter] = low
        total += dot3(pt_t_high[quarter], pt_t_low[quarter], high, low)
    m_own[...] = m_own[...] - 2.0 * total.reshape(32, 8, 256)
    m_in[place] = m_own[place]

    for which, device_id in plane:
        pltpu.make_async_remote_copy(
            src_ref=m_own.at[which],
            dst_ref=m_in.at[place],
            send_sem=m_send,
            recv_sem=m_recv,
            device_id=device_id,
            device_id_type=MESH,
        ).start()

    @pl.loop(0, 4)
    def _(i):
        rows = pl.ds(pl.multiple_of(256 * i, 256), 256)
        total = jnp.zeros((256, 256), F32)
        for j in range(4):
            total += dot3(t_high[j, rows], t_low[j, rows], p_col_high[j], p_col_low[j])
        product[pl.ds(2 * i, 2)] = total.reshape(2, 2, 64, 256)

    d_copy.wait()
    high, low = split(d_raw[...])
    d_high[...] = high
    d_low[...] = low

    to_pair = pltpu.make_async_remote_copy(
        src_ref=product.at[:, 1 - core],
        dst_ref=sibling,
        send_sem=sib_send,
        recv_sem=sib_recv,
        device_id=(row, chip * 2 + 1 - core),
        device_id_type=MESH,
    )
    to_pair.start()
    to_pair.wait_recv()
    for i in range(8):
        pair_sum[i] = product[i, core] + sibling[i]

    def to_chip(step, half):
        return pltpu.make_async_remote_copy(
            src_ref=pair_sum.at[half * 4 + lax.rem(x + step, 4)],
            dst_ref=pair_in.at[half * 4 + x],
            send_sem=pair_send.at[half * 4 + step],
            recv_sem=pair_recv.at[half * 4 + x],
            device_id=(row, z_lo * 8 + lax.rem(in_plane + 2 * step, 8)),
            device_id_type=MESH,
        )

    for half in range(2):
        for step in (2, 1, 3):
            to_chip(step, half).start()

    whole(m_in, 31, m_recv)

    total = m_in[0]
    for i in range(1, 32):
        total += m_in[i]
    m_sum[...] = total
    m_plane[z] = total

    for device_id in along_z_ids:
        pltpu.make_async_remote_copy(
            src_ref=m_sum,
            dst_ref=m_plane.at[z],
            send_sem=z_send,
            recv_sem=z_recv,
            device_id=device_id,
            device_id_type=MESH,
        ).start()

    whole(m_plane, 7, z_recv)

    total = m_plane[0]
    for i in range(1, 8):
        total += m_plane[i]
    high, low = split(jnp.concatenate([total, total], axis=0))
    total = dot3(high, low, d_high[...], d_low[...])[0:8]
    md_own[...] = total
    md[place] = total

    for _, device_id in plane:
        pltpu.make_async_remote_copy(
            src_ref=md_own,
            dst_ref=md.at[place],
            send_sem=out_send,
            recv_sem=out_recv,
            device_id=device_id,
            device_id_type=MESH,
        ).start()

    for half in range(2):
        for step in (1, 2, 3):
            which = half * 4 + lax.rem(x + step, 4)
            pltpu.make_async_copy(p_own, pair_in.at[which], pair_recv.at[which]).wait()
        reduced = pair_sum[half * 4 + x]
        for step in (1, 2, 3):
            reduced += pair_in[half * 4 + lax.rem(x + step, 4)]
        x_sum[half] = reduced

    to_other = pltpu.make_async_remote_copy(
        src_ref=x_sum.at[1 - z_lo],
        dst_ref=x_in,
        send_sem=other_send,
        recv_sem=other_recv,
        device_id=(row, (1 - z_lo) * 8 + in_plane),
        device_id_type=MESH,
    )
    to_other.start()
    to_other.wait_recv()
    reduced = x_sum[z_lo] + x_in[...]
    high, low = split(a_own[...] - 2.0 * reduced)
    solved_ref[...] = dot3(high, low, d_high[...], d_low[...])
    c_copy.wait()

    @pl.when(jnp.logical_not(diagonal))
    def _():
        spread(0).wait_send()

    spread(1).wait_send()
    for i in range(2):
        across(i).wait_send()
        for step in (1, 3):
            along_y(i, step).wait_send()
            along_z(i, step).wait_send()
            onward(i, step).wait_send()
    to_sibling(0).wait_send()
    to_partner().wait_send()
    for step in (1, 2, 3):
        to_row(0, step).wait_send()
        to_row(1, step).wait_send()
    to_pair.wait_send()
    to_other.wait_send()
    for step in (1, 2, 3):
        to_chip(step, 0).wait_send()
        to_chip(step, 1).wait_send()

    @pl.loop(1, 8)
    def _(step):
        to_sibling(step).wait_send()

    whole(m_in, 31, m_send)
    whole(m_plane, 7, z_send)
    whole(md, 31, out_send)

    whole(md, 31, out_recv)

    corner_ref[...] = c_raw[...] - md[...].reshape(256, 256).T


def store(solved_ref, corner_ref, solved_out, corner_out, solved_sem, corner_sem):
    corner = pltpu.make_async_copy(corner_ref, corner_out, corner_sem)
    solved = pltpu.make_async_copy(solved_ref, solved_out, solved_sem)
    corner.start()
    solved.start()
    corner.wait()
    solved.wait()


def body(*arrays):
    hbm = pl.BlockSpec(memory_space=pltpu.HBM)
    vmem = pl.BlockSpec(memory_space=pltpu.VMEM)
    dma = pltpu.SemaphoreType.DMA
    results = pl.pallas_call(
        kernel,
        out_shape=(
            jax.ShapeDtypeStruct((64, 256), F32),
            jax.ShapeDtypeStruct((256, 256), F32),
        ),
        in_specs=[hbm] * 5,
        out_specs=(vmem, vmem),
        scratch_shapes=[
            pltpu.VMEM((1024, 1024), F32),
            pltpu.VMEM((4, 1024, 256), BF16),
            pltpu.VMEM((4, 1024, 256), BF16),
            pltpu.VMEM((64, 256), F32),
            pltpu.VMEM((64, 256), F32),
            pltpu.VMEM((256, 256), F32),
            pltpu.VMEM((256, 256), F32),
            pltpu.VMEM((256, 256), BF16),
            pltpu.VMEM((256, 256), BF16),
            pltpu.VMEM((4, 256, 256), F32),
            pltpu.VMEM((16, 64, 256), F32),
            pltpu.VMEM((256, 1024), BF16),
            pltpu.VMEM((256, 1024), BF16),
            pltpu.VMEM((4, 256, 256), BF16),
            pltpu.VMEM((4, 256, 256), BF16),
            pltpu.VMEM((4, 256, 256), BF16),
            pltpu.VMEM((4, 256, 256), BF16),
            pltpu.VMEM((8, 2, 64, 256), F32),
            pltpu.VMEM((8, 64, 256), F32),
            pltpu.VMEM((8, 64, 256), F32),
            pltpu.VMEM((8, 64, 256), F32),
            pltpu.VMEM((2, 64, 256), F32),
            pltpu.VMEM((64, 256), F32),
            pltpu.VMEM((32, 8, 256), F32),
            pltpu.VMEM((32, 8, 256), F32),
            pltpu.VMEM((8, 256), F32),
            pltpu.VMEM((8, 8, 256), F32),
            pltpu.VMEM((8, 256), F32),
            pltpu.VMEM((32, 8, 256), F32),
            dma((8,)),
            dma((2,)),
            dma((4, 4)),
            dma((2, 4)),
            dma((2, 4)),
            dma((2, 4)),
            dma((2,)),
            dma((8,)),
            dma((8,)),
            dma((16,)),
            dma(()),
            dma(()),
            dma((8,)),
            dma((8,)),
            dma(()),
            dma(()),
            dma(()),
            dma(()),
            dma(()),
            dma(()),
            dma(()),
            dma(()),
        ],
        compiler_params=pltpu.CompilerParams(
            collective_id=0, has_side_effects=True, vmem_limit_bytes=32 * 1024 * 1024
        ),
        name="adjoint_panel",
    )(*(pltpu.with_memory_space_constraint(x, pltpu.HBM) for x in arrays))
    return pl.pallas_call(
        store,
        out_shape=(
            jax.ShapeDtypeStruct((64, 256), F32),
            jax.ShapeDtypeStruct((256, 256), F32),
        ),
        in_specs=[pl.BlockSpec(memory_space=pl.ANY)] * 2,
        out_specs=(hbm, hbm),
        scratch_shapes=[dma(()), dma(())],
        name="store_results",
    )(*results)


def solution(mesh):
    placed = (P("row", "col"), P(("row", "col"), None), P(("row", "col"), None), P(), P())
    return jax.shard_map(
        body, mesh=mesh, in_specs=placed, out_specs=(P(("row", "col"), None), P()), check_vma=False
    )
```

```python
import functools

import jax
import jax.numpy as jnp
from jax import lax
from jax.experimental import pallas as pl
from jax.experimental.pallas import tpu as pltpu
from jax.sharding import PartitionSpec as P

MESH = pl.DeviceIdType.MESH
F32 = jnp.float32
BF16 = jnp.bfloat16


def split(value):
    high = value.astype(BF16)
    return high, (value - high.astype(F32)).astype(BF16)


def dot3(a_high, a_low, b_high, b_low):
    dot = functools.partial(jnp.dot, preferred_element_type=F32)
    return dot(a_high, b_high) + (dot(a_high, b_low) + dot(a_low, b_high))


def kernel(
    t_hbm, p_hbm, a_hbm, d_hbm, c_hbm, solved_ref, corner_ref,
    t_raw, t_high, t_low, p_own, a_own, d_raw, c_raw, d_high, d_low,
    p_col, p_row, pt_high, pt_low, pt_t_high, pt_t_low, p_col_high, p_col_low, product,
    sibling, pair_sum, pair_in, x_sum, x_in, m_own, m_in, m_sum, m_plane, md_own, md,
    local_sem, spread_send, col_recv, z_relay_send, y_relay_send, onward_send,
    row_send, row_fwd, row_recv, sib_send, sib_recv, pair_send, pair_recv, other_send, other_recv,
    m_send, m_recv, z_send, z_recv, out_send, out_recv,
):
    row, col = lax.axis_index("row"), lax.axis_index("col")
    y, z_hi = lax.div(row, 4), lax.rem(row, 4)
    z_lo, in_plane, core = lax.div(col, 8), lax.rem(col, 8), lax.rem(col, 2)
    chip = lax.div(col, 2)
    z = z_hi * 2 + z_lo
    x, place = lax.div(in_plane, 2), y * 8 + in_plane
    far_y, far_z, next_z, last_z = (
        lax.rem(y + 2, 4), lax.rem(z_hi + 2, 4), lax.rem(z_hi + 1, 4), lax.rem(z_hi + 3, 4)
    )

    def opposite(which):
        return lax.rem(lax.div(which, 4) + 2, 4) * 4 + lax.rem(which + 2, 4)

    rows = [lax.rem(y + step, 4) for step in range(4)]
    places = [lax.rem(in_plane + step, 8) for step in range(8)]
    plane = [
        (rows[i] * 8 + places[j], (rows[i] * 4 + z_hi, z_lo * 8 + places[j]))
        for i in (2, 1, 3, 0)
        for j in (4, 5, 3, 2, 6, 1, 7, 0)
        if i or j
    ]
    along_z_ids = []
    for step in (4, 3, 5, 2, 6, 1, 7):
        to_z = lax.rem(z + step, 8)
        along_z_ids.append((y * 4 + lax.div(to_z, 2), lax.rem(to_z, 2) * 8 + in_plane))

    def whole(pieces, count, sem):
        pltpu.make_async_copy(
            pieces.at[pl.ds(0, count)], pieces.at[pl.ds(0, count)], sem
        ).wait()

    slabs = [
        pltpu.make_async_copy(
            t_hbm.at[pl.ds(256 * i, 256)], t_raw.at[pl.ds(256 * i, 256)], local_sem.at[i]
        )
        for i in range(4)
    ]
    p_copy = pltpu.make_async_copy(p_hbm, p_own, local_sem.at[4])
    a_copy = pltpu.make_async_copy(a_hbm, a_own, local_sem.at[5])
    d_copy = pltpu.make_async_copy(d_hbm, d_raw, local_sem.at[6])
    c_copy = pltpu.make_async_copy(c_hbm, c_raw, local_sem.at[7])
    for copy in [p_copy, a_copy] + slabs + [d_copy, c_copy]:
        copy.start()

    barrier = pltpu.get_barrier_semaphore()

    def greet(device_id):
        pl.semaphore_signal(barrier, inc=1, device_id=device_id, device_id_type=MESH)

    diagonal = row == col

    @pl.when(jnp.logical_not(diagonal))
    def _():
        greet((col, row))

    greet((col, opposite(row)))

    for device_id in along_z_ids:
        greet(device_id)

    for _, device_id in plane:
        greet(device_id)

    p_copy.wait()
    p_row[col] = p_own[...]
    pl.semaphore_wait(barrier, 2 + 7 + 31 - diagonal.astype(jnp.int32))

    def piece(quarter, which):
        return p_col.at[quarter, pl.ds(pl.multiple_of(64 * which, 64), 64)]

    def arrived(quarter, which):
        pltpu.make_async_copy(p_own, piece(quarter, which), col_recv.at[quarter, which]).wait()

    own_piece = piece(lax.div(col, 4), lax.rem(col, 4))
    own_recv = col_recv.at[lax.div(col, 4), lax.rem(col, 4)]

    def spread(i):
        return pltpu.make_async_remote_copy(
            src_ref=p_own,
            dst_ref=own_piece,
            send_sem=spread_send.at[i],
            recv_sem=own_recv,
            device_id=((col, opposite(col))[i], row),
            device_id_type=MESH,
        )

    @pl.when(diagonal)
    def _():
        pltpu.make_async_copy(p_own, own_piece, own_recv).start()

    @pl.when(jnp.logical_not(diagonal))
    def _():
        spread(0).start()

    spread(1).start()

    held = ((y, z_hi), (far_y, far_z))
    passed = ((y, last_z), (far_y, next_z))

    def relay(source, send_sem, to_y, to_z):
        return pltpu.make_async_remote_copy(
            src_ref=piece(*source),
            dst_ref=piece(*source),
            send_sem=send_sem,
            recv_sem=col_recv.at[source[0], source[1]],
            device_id=(to_y * 4 + to_z, col),
            device_id_type=MESH,
        )

    def along_z(i, step):
        return relay(held[i], z_relay_send.at[i, step], y, lax.rem(z_hi + step, 4))

    def along_y(i, step):
        return relay(held[i], y_relay_send.at[i, step], lax.rem(y + step, 4), z_hi)

    def onward(i, step):
        return relay(passed[i], onward_send.at[i, step], lax.rem(y + step, 4), z_hi)

    def to_partner():
        return pltpu.make_async_remote_copy(
            src_ref=p_own,
            dst_ref=p_row.at[col],
            send_sem=row_send.at[0],
            recv_sem=row_recv.at[col],
            device_id=(row, (1 - z_lo) * 8 + in_plane),
            device_id_type=MESH,
        )

    def to_row(half, step):
        which = lax.rem(z_lo + half, 2) * 8 + in_plane
        block = p_row.at[which]
        return pltpu.make_async_remote_copy(
            src_ref=block,
            dst_ref=block,
            send_sem=row_send.at[half * 4 + step],
            recv_sem=row_recv.at[which],
            device_id=(row, z_lo * 8 + lax.rem(in_plane + 2 * step, 8)),
            device_id_type=MESH,
        )

    def to_sibling(step):
        which = lax.rem(chip + step, 8) * 2 + core
        block = p_row.at[which]
        return pltpu.make_async_remote_copy(
            src_ref=block,
            dst_ref=block,
            send_sem=row_fwd.at[step],
            recv_sem=row_recv.at[which],
            device_id=(row, chip * 2 + 1 - core),
            device_id_type=MESH,
        )

    def row_arrived(which):
        pltpu.make_async_copy(p_own, p_row.at[which], row_recv.at[which]).wait()

    to_partner().start()
    to_sibling(0).start()

    a_copy.wait()
    p_high, p_low = split(p_own[...])
    a_high, a_low = split(a_own[...])
    m_own[...] = dot3(p_high.T, p_low.T, a_high, a_low).reshape(32, 8, 256)
    for i in range(4):
        slabs[i].wait()

        @pl.loop(0, 4)
        def _(j, i=i):
            rows = pl.ds(256 * i, 256)
            high, low = split(t_raw[rows, pl.ds(pl.multiple_of(256 * j, 256), 256)])
            t_high[j, rows] = high
            t_low[j, rows] = low

    d_copy.wait()
    high, low = split(d_raw[...])
    d_high[...] = high
    d_low[...] = low

    for step in (2, 1, 3):
        to_row(0, step).start()
    row_arrived((1 - z_lo) * 8 + in_plane)
    for step in (2, 1, 3):
        to_row(1, step).start()
    to_sibling(4).start()

    for i in range(2):
        arrived(*held[i])
        for step in (1, 3):
            along_z(i, step).start()
        for step in (2, 1, 3):
            along_y(i, step).start()

    for i in range(2):
        arrived(*passed[i])
        for step in (1, 3):
            onward(i, step).start()

    for step in (1, 2, 3, 5, 6, 7):
        row_arrived(lax.rem(chip + step, 8) * 2 + core)
        to_sibling(step).start()

    for i in range(4):
        for step in (0, 1):
            row_arrived(4 * i + 2 * step + 1 - core)
        high, low = split(p_row[pl.ds(4 * i, 4)].reshape(256, 256))
        pt_high[:, pl.ds(256 * i, 256)] = high.T
        pt_low[:, pl.ds(256 * i, 256)] = low.T

    @pl.loop(0, 4)
    def _(j):
        high, low = split(dot3(pt_high[...], pt_low[...], t_high[j], t_low[j]))
        pt_t_high[j] = high
        pt_t_low[j] = low

    total = jnp.zeros((256, 256), F32)
    for step, rest in ((0, (1, 2)), (2, (0, 3)), (1, (0, 2, 1, 3)), (3, (0, 2, 1, 3))):
        quarter = lax.rem(y + step, 4)
        for i in rest:
            arrived(quarter, lax.rem(z_hi + i, 4))
        high, low = split(p_col[quarter])
        p_col_high[quarter] = high
        p_col_low[quarter] = low
        total += dot3(pt_t_high[quarter], pt_t_low[quarter], high, low)
    m_own[...] = m_own[...] - 2.0 * total.reshape(32, 8, 256)
    m_in[place] = m_own[place]

    for which, device_id in plane:
        pltpu.make_async_remote_copy(
            src_ref=m_own.at[which],
            dst_ref=m_in.at[place],
            send_sem=m_send,
            recv_sem=m_recv,
            device_id=device_id,
            device_id_type=MESH,
        ).start()

    def to_pair(i):
        return pltpu.make_async_remote_copy(
            src_ref=product.at[pl.ds(2 * i, 2), 1 - core],
            dst_ref=sibling.at[pl.ds(2 * i, 2)],
            send_sem=sib_send.at[i],
            recv_sem=sib_recv.at[i],
            device_id=(row, chip * 2 + 1 - core),
            device_id_type=MESH,
        )

    @pl.loop(0, 4)
    def _(i):
        rows = pl.ds(pl.multiple_of(256 * i, 256), 256)
        total = jnp.zeros((256, 256), F32)
        for j in range(4):
            total += dot3(t_high[j, rows], t_low[j, rows], p_col_high[j], p_col_low[j])
        product[pl.ds(2 * i, 2)] = total.reshape(2, 2, 64, 256)
        to_pair(i).start()

    for i in range(4):
        to_pair(i).wait_recv()
        for j in (2 * i, 2 * i + 1):
            pair_sum[j] = product[j, core] + sibling[j]

    def to_chip(step, half):
        return pltpu.make_async_remote_copy(
            src_ref=pair_sum.at[half * 4 + lax.rem(x + step, 4)],
            dst_ref=pair_in.at[half * 4 + x],
            send_sem=pair_send.at[half * 4 + step],
            recv_sem=pair_recv.at[half * 4 + x],
            device_id=(row, z_lo * 8 + lax.rem(in_plane + 2 * step, 8)),
            device_id_type=MESH,
        )

    for half in range(2):
        for step in (2, 1, 3):
            to_chip(step, half).start()

    whole(m_in, 31, m_recv)

    total = m_in[0]
    for i in range(1, 32):
        total += m_in[i]
    m_sum[...] = total
    m_plane[z] = total

    for device_id in along_z_ids:
        pltpu.make_async_remote_copy(
            src_ref=m_sum,
            dst_ref=m_plane.at[z],
            send_sem=z_send,
            recv_sem=z_recv,
            device_id=device_id,
            device_id_type=MESH,
        ).start()

    whole(m_plane, 7, z_recv)

    total = m_plane[0]
    for i in range(1, 8):
        total += m_plane[i]
    high, low = split(jnp.concatenate([total, total], axis=0))
    total = dot3(high, low, d_high[...], d_low[...])[0:8]
    md_own[...] = total
    md[place] = total

    for _, device_id in plane:
        pltpu.make_async_remote_copy(
            src_ref=md_own,
            dst_ref=md.at[place],
            send_sem=out_send,
            recv_sem=out_recv,
            device_id=device_id,
            device_id_type=MESH,
        ).start()

    for half in range(2):
        for step in (1, 2, 3):
            which = half * 4 + lax.rem(x + step, 4)
            pltpu.make_async_copy(p_own, pair_in.at[which], pair_recv.at[which]).wait()
        reduced = pair_sum[half * 4 + x]
        for step in (1, 2, 3):
            reduced += pair_in[half * 4 + lax.rem(x + step, 4)]
        x_sum[half] = reduced

    to_other = pltpu.make_async_remote_copy(
        src_ref=x_sum.at[1 - z_lo],
        dst_ref=x_in,
        send_sem=other_send,
        recv_sem=other_recv,
        device_id=(row, (1 - z_lo) * 8 + in_plane),
        device_id_type=MESH,
    )
    to_other.start()
    to_other.wait_recv()
    reduced = x_sum[z_lo] + x_in[...]
    high, low = split(a_own[...] - 2.0 * reduced)
    solved_ref[...] = dot3(high, low, d_high[...], d_low[...])
    c_copy.wait()

    @pl.when(jnp.logical_not(diagonal))
    def _():
        spread(0).wait_send()

    spread(1).wait_send()
    for i in range(2):
        for step in (1, 2, 3):
            along_y(i, step).wait_send()
        for step in (1, 3):
            along_z(i, step).wait_send()
            onward(i, step).wait_send()
    to_sibling(0).wait_send()
    to_partner().wait_send()
    for step in (1, 2, 3):
        to_row(0, step).wait_send()
        to_row(1, step).wait_send()
    for i in range(4):
        to_pair(i).wait_send()
    to_other.wait_send()
    for step in (1, 2, 3):
        to_chip(step, 0).wait_send()
        to_chip(step, 1).wait_send()

    @pl.loop(1, 8)
    def _(step):
        to_sibling(step).wait_send()

    whole(m_in, 31, m_send)
    whole(m_plane, 7, z_send)
    whole(md, 31, out_send)

    whole(md, 31, out_recv)

    corner_ref[...] = c_raw[...] - md[...].reshape(256, 256).T


def body(*arrays):
    hbm = pl.BlockSpec(memory_space=pltpu.HBM)
    vmem = pl.BlockSpec(memory_space=pltpu.VMEM)
    dma = pltpu.SemaphoreType.DMA
    return pl.pallas_call(
        kernel,
        out_shape=(
            jax.ShapeDtypeStruct((64, 256), F32),
            jax.ShapeDtypeStruct((256, 256), F32),
        ),
        in_specs=[hbm] * 5,
        out_specs=(vmem, vmem),
        scratch_shapes=[
            pltpu.VMEM((1024, 1024), F32),
            pltpu.VMEM((4, 1024, 256), BF16),
            pltpu.VMEM((4, 1024, 256), BF16),
            pltpu.VMEM((64, 256), F32),
            pltpu.VMEM((64, 256), F32),
            pltpu.VMEM((256, 256), F32),
            pltpu.VMEM((256, 256), F32),
            pltpu.VMEM((256, 256), BF16),
            pltpu.VMEM((256, 256), BF16),
            pltpu.VMEM((4, 256, 256), F32),
            pltpu.VMEM((16, 64, 256), F32),
            pltpu.VMEM((256, 1024), BF16),
            pltpu.VMEM((256, 1024), BF16),
            pltpu.VMEM((4, 256, 256), BF16),
            pltpu.VMEM((4, 256, 256), BF16),
            pltpu.VMEM((4, 256, 256), BF16),
            pltpu.VMEM((4, 256, 256), BF16),
            pltpu.VMEM((8, 2, 64, 256), F32),
            pltpu.VMEM((8, 64, 256), F32),
            pltpu.VMEM((8, 64, 256), F32),
            pltpu.VMEM((8, 64, 256), F32),
            pltpu.VMEM((2, 64, 256), F32),
            pltpu.VMEM((64, 256), F32),
            pltpu.VMEM((32, 8, 256), F32),
            pltpu.VMEM((32, 8, 256), F32),
            pltpu.VMEM((8, 256), F32),
            pltpu.VMEM((8, 8, 256), F32),
            pltpu.VMEM((8, 256), F32),
            pltpu.VMEM((32, 8, 256), F32),
            dma((8,)),
            dma((2,)),
            dma((4, 4)),
            dma((2, 4)),
            dma((2, 4)),
            dma((2, 4)),
            dma((8,)),
            dma((8,)),
            dma((16,)),
            dma((4,)),
            dma((4,)),
            dma((8,)),
            dma((8,)),
            dma(()),
            dma(()),
            dma(()),
            dma(()),
            dma(()),
            dma(()),
            dma(()),
            dma(()),
        ],
        compiler_params=pltpu.CompilerParams(
            collective_id=0, has_side_effects=True, vmem_limit_bytes=32 * 1024 * 1024
        ),
        name="adjoint_panel",
    )(*(pltpu.with_memory_space_constraint(x, pltpu.HBM) for x in arrays))


def solution(mesh):
    placed = (P("row", "col"), P(("row", "col"), None), P(("row", "col"), None), P(), P())
    return jax.shard_map(
        body, mesh=mesh, in_specs=placed, out_specs=(P(("row", "col"), None), P()), check_vma=False
    )
```
